256 devices in a mesh: gx: 8 (over z), gz: 16 (over x, y), col: 2 (over core).
Axes of the slice: x: 4, y: 4, z: 8, core: 2. Of those that a mesh axis runs over, the one named last changes fastest.
Arguments:
- density: float32 [256, 256, 256], P('gx', 'gz', 'col'), may hold values from 0.5 to 2
- momentum: float32 [3, 256, 256, 256], P(None, 'gx', 'gz', 'col'), may hold values from -6 to 6
- adjoint: float32 [5, 256, 256, 256], P(None, 'gx', 'gz', 'col'), may hold values from -6 to 6
- objective: float32 [5, 256, 256, 256], P(None, 'gx', 'gz', 'col'), may hold values from -6 to 6
- flux_jac: float32 [3, 5, 5], replicated, may hold values from -2.5 to 2.5
- wall_owner: int32 [2097152, 1], P(('gx', 'gz', 'col')), may hold values from 0 to 255; in each aligned block of 8192 rows (0 to 8191, 8192 to 16383, ...) at most 64 rows name the same one
- wall_node: int32 [2097152], P(('gx', 'gz', 'col')), may hold values from 0 to 8191
- wall_cell: int32 [2097152], P(('gx', 'gz', 'col')), may hold values from 0 to 65535
- wall_weight: float32 [2097152], P(('gx', 'gz', 'col')), may hold values from 0.5 to 2
- wall_normal: float32 [3, 2097152], P(None, ('gx', 'gz', 'col')), may hold values from -6 to 6
- shell_source: float32 [3, 2097152], P(None, ('gx', 'gz', 'col')), may hold values from -6 to 6
- shell_diag: float32 [3, 2097152], P(None, ('gx', 'gz', 'col')), may hold values from 0.5 to 2
- shell_coupling: float32 [3, 3, 2097152], P(None, None, ('gx', 'gz', 'col')), may hold values from -4 to 4
Outputs:
- fluid_out: float32 [5, 256, 256, 256], P(None, 'gx', 'gz', 'col')
- shell_adjoint: float32 [3, 2097152], P(None, ('gx', 'gz', 'col'))
The draws below stay inside these ranges and needn't reach their ends.
Inputs may be any that keep to these rules, and one draw needn't show every extreme that they name: `wall_owner`: at most 64 of the rows of one device name the same owner.
All inputs are finite; a program needn't handle non-finite values.
Results may differ from the reference program's by a relative error of at most 0.00011.
Values sent between devices are 32-bit elements; how exact they have to be, the bound alone decides.
A program may use at most 128 MiB of HBM per device.

```python
import math
import jax
import jax.numpy as jnp
import numpy as np
from jax import lax

CX = 32
CZ = 16
SP = 128
W_DEV = 8192
NODE_DEV = 8192
NX = 256
NZ = 256
SPAN = 256
NODES = 2097152
CAP = 64
N_GZ = 16
N_COL = 2
DEVICES = 256


def touch_ends(array, own_key, least, top_value):
    extent = array.shape
    index_at = [jax.random.randint(jax.random.fold_in(own_key, axis), (), 0, extent[axis]) for axis in range(len(extent))]
    array = array.at[tuple(index_at)].set(least)
    longest = extent.index(max(extent))
    index_at[longest] = (index_at[longest] + 1) % extent[longest]
    return array.at[tuple(index_at)].set(top_value)


def block_levels(stream_key, extent, cuts, low, top_value):
    level = 1.0
    for position, shards_of in cuts:
        draws = jax.random.uniform(jax.random.fold_in(jax.random.fold_in(stream_key, 6), position), (shards_of,), jnp.float32, low / len(cuts), top_value / len(cuts))
        level = level * jnp.repeat(jnp.exp(draws), extent[position] // shards_of).reshape((-1,) + (1,) * (len(extent) - 1 - position))
    return level


def assign_block(stream_key, own, number, rows, count, top, most, lean):
    sequence = jax.random.permutation(stream_key, count)
    heavy_load, common = load_shares(count, rows * top, most, lean, True), load_shares(count, rows * top, most, lean, False)
    places = jnp.arange(count)

    def named(sizes, offset_by):
        used = int((sizes > 0).sum())
        fixed = max(1, used // 4)
        shifted = fixed + (places - fixed + offset_by * (used - fixed)) % max(1, count - fixed)
        return jnp.zeros((count,), jnp.int32).at[sequence[jnp.where(places < fixed, places, shifted)]].set(jnp.asarray(sizes, jnp.int32))

    sizes = jnp.where(number % 4 == 0, named(heavy_load, number // 4), named(common, number - number // 4 - 1))
    mixed = jax.random.permutation(jax.random.fold_in(own, 3), count)
    donor, sink = mixed[0:count // 2 * 2:2], mixed[1:count // 2 * 2:2]
    slack = jnp.minimum(sizes[donor] - 1, most - sizes[sink]) // 2
    slack = jnp.where((donor == sequence[0]) | (sink == sequence[0]) | (sizes[sink] == 0), 0, jnp.maximum(slack, 0))
    shifted = jax.random.randint(jax.random.fold_in(own, 4), (count // 2,), 0, 1 << 20) % (slack + 1)
    sizes = sizes.at[donor].add(-shifted).at[sink].add(shifted)
    items = jnp.searchsorted(jnp.cumsum(sizes), jnp.arange(rows * top), side="right").astype(jnp.int32)
    grid = items.reshape(top, rows).T
    grid = grid[jax.random.permutation(jax.random.fold_in(own, 1), rows)]
    offset_by = jax.random.randint(jax.random.fold_in(own, 2), (rows, 1), 0, top)
    return jnp.take_along_axis(grid, (jnp.arange(top)[None, :] + offset_by) % top, axis=1)


def load_shares(number_of, total, bound, skew, full):
    weights = [(1 << 20) // math.isqrt(standing ** skew) + 1 for standing in range(1, number_of + 1)]
    largest = bound if full else min(bound, max(-(-total // number_of), total * weights[0] // sum(weights)))
    least = 1 if total - largest >= number_of - 1 else 0
    counts, rest = [largest] + [least] * (number_of - 1), total - largest - least * (number_of - 1)
    while rest > 0:
        movable = [i for i in range(1, number_of) if counts[i] < largest] or [i for i in range(1, number_of) if counts[i] < bound]
        pool, budget = sum([weights[i] for i in movable]), rest
        for i in movable:
            addition = min(bound - counts[i], max(1, budget * weights[i] // pool), rest)
            counts[i] = counts[i] + addition
            rest = rest - addition
    return np.array(counts)


def gaussian(key, extent, deviation, most, split=(), held_as=jnp.bfloat16):
    loudness = block_levels(key, extent, split, -0.22, 0.18) if split else 1.0
    values = jax.random.normal(key, extent, jnp.float32) * deviation * loudness
    return jnp.minimum(jnp.maximum(values, -most), most).astype(held_as)


def setup_inputs(seed: int = 0) -> dict:
    splits = jax.random.split(jax.random.key(seed), 14)
    density = jnp.clip(jnp.exp(math.log(2.0) - 1.3862944 * jax.random.uniform(splits[0], (NX, NZ, SPAN), jnp.float32) ** block_levels(splits[0], (NX, NZ, SPAN), ((0, 8), (1, 16), (2, 2)), -0.2, 0.2)), 0.5, 2.0)
    momentum = gaussian(splits[1], (3, NX, NZ, SPAN), 1.0, 6.0, ((1, 8), (2, 16), (3, 2)), jnp.float32)
    adjoint = gaussian(splits[2], (5, NX, NZ, SPAN), 1.0, 6.0, ((1, 8), (2, 16), (3, 2)), jnp.float32)
    objective = gaussian(splits[3], (5, NX, NZ, SPAN), 1.0, 6.0, ((1, 8), (2, 16), (3, 2)), jnp.float32)
    flux_jac = gaussian(splits[4], (3, 5, 5), 5 ** -0.5, 2.5, (), jnp.float32)
    wall_owner_keys = jax.random.split(jax.random.fold_in(splits[5], 1), (DEVICES * W_DEV) // W_DEV)
    wall_owner_turns = jax.random.permutation(jax.random.fold_in(splits[5], 3), (DEVICES * W_DEV) // W_DEV)
    wall_owner = jax.vmap(lambda own, number: assign_block(jax.random.fold_in(splits[5], 2), own, number, W_DEV, DEVICES, 1, CAP, 2))(wall_owner_keys, wall_owner_turns).reshape((DEVICES * W_DEV, 1))
    wall_node = touch_ends(jax.random.randint(splits[6], (DEVICES * W_DEV,), 0, NODE_DEV), jax.random.fold_in(splits[6], 1), 0, NODE_DEV - 1).astype(jnp.int32)
    wall_cell = touch_ends(jax.random.randint(splits[7], (DEVICES * W_DEV,), 0, CX * CZ * SP), jax.random.fold_in(splits[7], 1), 0, (CX * CZ * SP) - 1).astype(jnp.int32)
    wall_weight = jnp.clip(jnp.exp(math.log(2.0) - 1.3862944 * jax.random.uniform(splits[8], (DEVICES * W_DEV,), jnp.float32) ** block_levels(splits[8], (DEVICES * W_DEV,), ((0, 256),), -0.2, 0.2)), 0.5, 2.0)
    wall_normal = gaussian(splits[9], (3, DEVICES * W_DEV), 1.0, 6.0, ((1, 256),), jnp.float32)
    shell_source = gaussian(splits[10], (3, NODES), 1.0, 6.0, ((1, 256),), jnp.float32)
    shell_diag = jnp.clip(jnp.exp(math.log(2.0) - 1.3862944 * jax.random.uniform(splits[11], (3, NODES), jnp.float32) ** block_levels(splits[11], (3, NODES), ((1, 256),), -0.2, 0.2)), 0.5, 2.0)
    shell_coupling = gaussian(splits[12], (3, 3, NODES), 0.3, 4.0, ((2, 256),), jnp.float32)
    return {"density": density, "momentum": momentum, "adjoint": adjoint, "objective": objective, "flux_jac": flux_jac, "wall_owner": wall_owner, "wall_node": wall_node, "wall_cell": wall_cell, "wall_weight": wall_weight, "wall_normal": wall_normal, "shell_source": shell_source, "shell_diag": shell_diag, "shell_coupling": shell_coupling}


step_tau = 0.25


def stencil(padded, velocity, flux_jac):
    nx = padded.shape[1] - 4
    nz = padded.shape[2] - 4
    ns = padded.shape[3] - 4
    sizes = [padded.shape[0], nx, nz, ns]
    total = jnp.zeros(sizes, jnp.float32)
    for direction in range(3):
        pieces = []
        for offset in (0, 1, 3, 4):
            start = [0, 2, 2, 2]
            start[direction + 1] = offset
            limit = [start[k] + sizes[k] for k in range(4)]
            pieces.append(lax.slice(padded, start, limit))
        delta = (8.0 * (pieces[1] - pieces[2]) - (pieces[0] - pieces[3])) / 12.0
        mixed = jnp.einsum('ji,jxzs->ixzs', flux_jac[direction], delta, precision=lax.Precision.HIGHEST)
        total = total + velocity[direction][None] * delta + mixed
    return total


def reference(density, momentum, adjoint, objective, flux_jac, wall_owner, wall_node, wall_cell, wall_weight, wall_normal, shell_source, shell_diag, shell_coupling):
    velocity = momentum / density[None]
    padded = jnp.pad(adjoint, ((0, 0), (2, 2), (2, 2), (2, 2)))
    middle = adjoint - step_tau * (stencil(padded, velocity, flux_jac) + objective)
    device = jnp.arange(DEVICES * W_DEV, dtype=jnp.int32) // W_DEV
    tile_x = device // (N_GZ * N_COL)
    tile_z = (device // N_COL) % N_GZ
    tile_s = device % N_COL
    xs = tile_x * CX + wall_cell // (CZ * SP)
    zs = tile_z * CZ + (wall_cell // SP) % CZ
    ss = tile_s * SP + wall_cell % SP
    pressure = middle[4, xs, zs, ss]
    traction = wall_weight[None] * wall_normal * pressure[None]
    nodes = (wall_owner[:, 0] * NODE_DEV + wall_node).astype(jnp.int32)
    loads = jnp.zeros((3, NODES), jnp.float32).at[:, nodes].add(traction) + shell_source
    shell = shell_diag * loads + jnp.einsum('ijn,jn->in', shell_coupling, loads, precision=lax.Precision.HIGHEST)
    returned = shell[:, nodes]
    source = wall_weight * jnp.sum(wall_normal * returned, 0)
    fluid_out = middle.at[4, xs, zs, ss].add(source)
    return fluid_out, shell
```

```python
import functools

import jax
import jax.numpy as jnp
from jax import lax
from jax.experimental import pallas as pl
from jax.experimental.pallas import tpu as pltpu
from jax.sharding import PartitionSpec as P

tau = 0.25
f32, bf16, i32 = jnp.float32, jnp.bfloat16, jnp.int32
MESH = pl.DeviceIdType.MESH
GX, GZ, COL = 8, 16, 2
CX, CZ, SP = 32, 16, 128
FACES, NODES = 8192, 8192
CHUNK = 1024
VMEM_LIMIT = 56 * 1024 * 1024


def vmem():
    return pl.BlockSpec(memory_space=pltpu.VMEM)


def split(x):
    high = x.astype(bf16).astype(f32)
    return high, x - high


def one_hot(rows, index):
    return lax.broadcasted_iota(i32, (rows, index.shape[1]), 0) == index


def as_bf16(mask):
    return jnp.where(mask, 1.0, 0.0).astype(bf16)


def dot(a, b):
    return jnp.dot(a, b, preferred_element_type=f32)


def dot_nt(a, b):
    return lax.dot_general(a, b, (((1,), (1,)), ((), ())), preferred_element_type=f32)


def owner_column(owner):
    return (owner % 2) * 128 + owner // 2


def slots_from(summed):
    return jnp.concatenate([summed[:, :128], summed[:, 128:]], 0).T


def order_kernel(owner_ref, node_ref, weight_ref, normal_ref, rank_ref, pay_ref, owners_ref, carry_ref, acc_ref):
    rows = lax.broadcasted_iota(i32, (256, 384), 0)
    cols = lax.broadcasted_iota(i32, (256, 384), 1)
    ahead = as_bf16((rows < cols) | (cols >= 256))
    carry_ref[...] = jnp.zeros_like(carry_ref)
    acc_ref[...] = jnp.zeros_like(acc_ref)

    def rank_step(block, _):
        at = pl.ds(pl.multiple_of(block * 256, 256), 256)
        mask = one_hot(256, owner_column(owner_ref[:, at]))
        chosen = as_bf16(mask)
        owners_ref[:, at] = chosen
        counts = dot(chosen, ahead)
        carry = carry_ref[...]
        before = counts[:, :256] + jnp.concatenate([carry, carry], 1)
        rank_ref[:, at] = jnp.sum(jnp.where(mask, before, 0.0), 0, keepdims=True).astype(i32)
        carry_ref[...] = carry + counts[:, 256:]
        return 0

    lax.fori_loop(0, FACES // 256, rank_step, 0)

    def place_step(block, _):
        at = pl.ds(pl.multiple_of(block * CHUNK, CHUNK), CHUNK)
        within = one_hot(64, rank_ref[:, at])
        weight = weight_ref[:, at]
        node = node_ref[:, at]
        pieces = []
        for k in range(3):
            pieces += split(weight * normal_ref[k : k + 1, at])
        pieces += [((node // 128) * 128).astype(f32), (node % 128).astype(f32)]
        stacked = jnp.concatenate(
            [jnp.where(within, piece, 0.0).astype(bf16) for piece in pieces], 0
        )
        acc_ref[...] += dot_nt(stacked, owners_ref[:, at])
        return 0

    lax.fori_loop(0, FACES // CHUNK, place_step, 0)
    for k in range(4):
        pay_ref[k] = slots_from(
            acc_ref[k * 128 : k * 128 + 64, :] + acc_ref[k * 128 + 64 : k * 128 + 128, :]
        )


def order(owner, node, weight, normal):
    return pl.pallas_call(
        order_kernel,
        out_shape=(
            jax.ShapeDtypeStruct((1, FACES), i32),
            jax.ShapeDtypeStruct((4, 128, 128), f32),
        ),
        in_specs=[vmem()] * 4,
        out_specs=(vmem(), vmem()),
        scratch_shapes=[
            pltpu.VMEM((256, FACES), bf16),
            pltpu.VMEM((256, 128), f32),
            pltpu.VMEM((512, 256), f32),
        ],
        compiler_params=pltpu.CompilerParams(vmem_limit_bytes=VMEM_LIMIT),
        name="order",
    )(owner, node, weight, normal)


def place():
    return lax.axis_index("gx"), lax.axis_index("gz"), lax.axis_index("col")


def greet(gx, gz, col):
    barrier = pltpu.get_barrier_semaphore()
    for k in range(1, GX):
        pl.semaphore_signal(barrier, inc=1, device_id=((gx + k) % GX, gz, col), device_id_type=MESH)
    for k in range(1, GZ):
        pl.semaphore_signal(barrier, inc=1, device_id=(gx, (gz + k) % GZ, col), device_id_type=MESH)
    pl.semaphore_signal(barrier, inc=1, device_id=(gx, gz, 1 - col), device_id_type=MESH)
    pl.semaphore_wait(barrier, GX + GZ - 1)


def remote(src, dst, sems, k, device):
    return pltpu.make_async_remote_copy(
        src_ref=src,
        dst_ref=dst,
        send_sem=sems.at[0, k],
        recv_sem=sems.at[1, k],
        device_id=device,
        device_id_type=MESH,
    )


def run(copies, local):
    for copy in copies:
        copy.start()
    local.start()
    for copy in copies:
        copy.wait_recv()
    local.wait()


def drain(copies):
    for copy in copies:
        copy.wait_send()


def exchange_kernel(lead, with_halo, forward, *refs):
    gx, gz, col = place()
    every = (slice(None),) * lead
    if with_halo:
        pay, adjoint, second, third, xlo, xhi, zlo, zhi, side, first, sems_z, sems_g, sems_c, local, sems_h = refs
    elif forward:
        pay, second, third, first, sems_z, sems_g, sems_c, local = refs
    else:
        answers, back, other, mixed, first, sems_z, sems_g, sems_c, local = refs
    greet(gx, gz, col)
    started = []
    sibling = (gx, gz, 1 - col)
    if with_halo:
        up, down = ((gx + 1) % GX, gz, col), ((gx + GX - 1) % GX, gz, col)
        high, low = (gx, (gz + 1) % GZ, col), (gx, (gz + GZ - 1) % GZ, col)
        halos = [
            remote(adjoint.at[:, CX - 2 : CX], xlo, sems_h, 0, up),
            remote(adjoint.at[:, 0:2], xhi, sems_h, 1, down),
            remote(adjoint.at[:, :, CZ - 2 : CZ], zlo, sems_h, 2, high),
            remote(adjoint.at[:, :, 0:2], zhi, sems_h, 3, low),
            remote(adjoint, side, sems_h, 4, sibling),
        ]
        for copy in halos:
            copy.start()
        started += halos
    if forward:
        copies = [
            remote(
                pay.at[every + ((gx + k) % GX,)], first.at[(gx,) + every], sems_z, k - 1, ((gx + k) % GX, gz, col)
            )
            for k in range(1, GX)
        ]
        run(copies, pltpu.make_async_copy(pay.at[every + (gx,)], first.at[(gx,) + every], local.at[0]))
        started += copies
        rows = (slice(None),) * (lead + 1)
        copies = [
            remote(
                first.at[rows + ((gz + k) % GZ,)], second.at[gz], sems_g, k - 1, (gx, (gz + k) % GZ, col)
            )
            for k in range(1, GZ)
        ]
        run(copies, pltpu.make_async_copy(first.at[rows + (gz,)], second.at[gz], local.at[1]))
        started += copies
        copy = remote(second, third, sems_c, 0, sibling)
        copy.start()
        copy.wait_recv()
        started += [copy]
    else:
        copy = remote(answers, other, sems_c, 0, sibling)
        copy.start()
        copy.wait_recv()
        started += [copy]
        half = lax.broadcasted_iota(i32, (GZ * GX, 128), 1) // 64
        mixed[...] = jnp.where(
            half == col,
            answers[...].reshape(GZ * GX, 128),
            pltpu.roll(other[...].reshape(GZ * GX, 128), 64, 1),
        ).reshape(GZ, GX, 128)
        copies = [
            remote(mixed.at[(gz + k) % GZ], first.at[:, gz], sems_g, k - 1, (gx, (gz + k) % GZ, col))
            for k in range(1, GZ)
        ]
        run(copies, pltpu.make_async_copy(mixed.at[gz], first.at[:, gz], local.at[1]))
        started += copies
        copies = [
            remote(first.at[(gx + k) % GX], back.at[gx], sems_z, k - 1, ((gx + k) % GX, gz, col))
            for k in range(1, GX)
        ]
        run(copies, pltpu.make_async_copy(first.at[gx], back.at[gx], local.at[0]))
        started += copies
    if with_halo:
        for copy in halos:
            copy.wait_recv()
    drain(started)


def semaphores(with_halo=False):
    dma = pltpu.SemaphoreType.DMA
    return [dma((2, GX - 1)), dma((2, GZ - 1)), dma((2, 1)), dma((2,))] + ([dma((2, 5))] if with_halo else [])


def comm_call(kernel, args, out_shapes, scratch, collective_id, name):
    return pl.pallas_call(
        kernel,
        out_shape=tuple(jax.ShapeDtypeStruct(shape, f32) for shape in out_shapes),
        in_specs=[vmem()] * len(args),
        out_specs=tuple(vmem() for _ in out_shapes),
        scratch_shapes=scratch,
        compiler_params=pltpu.CompilerParams(
            collective_id=collective_id, has_side_effects=True, vmem_limit_bytes=VMEM_LIMIT
        ),
        name=name,
    )(*args)


def exchange_first(pay, adjoint):
    return comm_call(
        functools.partial(exchange_kernel, 1, True, True),
        (pay, adjoint),
        [(GZ, GX, 4, 128)] * 2 + [(5, 2, CZ, SP)] * 2 + [(5, CX, 2, SP)] * 2 + [(5, CX, CZ, SP)],
        [pltpu.VMEM((GX, 4, GZ, 128), f32)] + semaphores(True),
        0,
        "exchange_first",
    )


def exchange_pressure(pay):
    return comm_call(
        functools.partial(exchange_kernel, 0, False, True),
        (pay,),
        [(GZ, GX, 128)] * 2,
        [pltpu.VMEM((GX, GZ, 128), f32)] + semaphores(),
        1,
        "exchange_pressure",
    )


def exchange_back(answers):
    return comm_call(
        functools.partial(exchange_kernel, 0, False, False),
        (answers,),
        [(GX, GZ, 128)],
        [pltpu.VMEM((GZ, GX, 128), f32), pltpu.VMEM((GZ, GX, 128), f32), pltpu.VMEM((GX, GZ, 128), f32)] + semaphores(),
        2,
        "exchange_back",
    )[0]


def fluid_kernel(
    flux, density, momentum, adjoint, objective, xlo, xhi, zlo, zhi, side,
    owner_ref, rank_ref, cell_ref, middle, plane_ref, pay_ref, ext, wide, acc_ref,
):
    gx, gz, col = place()
    lane = lax.broadcasted_iota(i32, (CZ, SP), 1)
    x_low = (gx > 0).astype(f32)
    x_high = (gx < GX - 1).astype(f32)
    z_low = (gz > 0).astype(f32)
    z_high = (gz < GZ - 1).astype(f32)
    s_low = (col > 0).astype(f32)
    s_high = (col < COL - 1).astype(f32)
    for j in range(5):
        ext[j, 2 : CX + 2] = adjoint[j]
        ext[j, 0:2] = xlo[j] * x_low
        ext[j, CX + 2 : CX + 4] = xhi[j] * x_high

    def plane_step(x, _):
        inverse = (tau / 12.0) / density[x]
        velocity = [momentum[d, x] * inverse for d in range(3)]
        deltas = []
        for j in range(5):
            here = adjoint[j, x]
            beside = side[j, x]
            dx = 8.0 * (ext[j, x + 1] - ext[j, x + 3]) - (ext[j, x] - ext[j, x + 4])
            tall = jnp.concatenate([zlo[j, x] * z_low, here, zhi[j, x] * z_high], 0)
            dz = 8.0 * (tall[1:17] - tall[3:19]) - (tall[0:16] - tall[4:20])
            low_side, high_side = beside * s_low, beside * s_high
            ds = 8.0 * (
                pltpu.roll(jnp.where(lane >= SP - 1, low_side, here), 1, 1)
                - pltpu.roll(jnp.where(lane < 1, high_side, here), SP - 1, 1)
            ) - (
                pltpu.roll(jnp.where(lane >= SP - 2, low_side, here), 2, 1)
                - pltpu.roll(jnp.where(lane < 2, high_side, here), SP - 2, 1)
            )
            deltas.append((dx, dz, ds))
        for i in range(5):
            total = velocity[0] * deltas[i][0] + velocity[1] * deltas[i][1] + velocity[2] * deltas[i][2]
            for d in range(3):
                for j in range(5):
                    total = total + (flux[d * 25 + j * 5 + i] * (tau / 12.0)) * deltas[j][d]
            value = adjoint[i, x] - (total + tau * objective[i, x])
            middle[i, x] = value
            if i == 4:
                plane_ref[pl.ds(pl.multiple_of(x * CZ, CZ), CZ), :] = value
        return 0

    lax.fori_loop(0, CX, plane_step, 0)

    turned = plane_ref[...].T
    high, low = split(turned)
    wide[0:128, :] = high.astype(bf16)
    wide[128:256, :] = low.astype(bf16)
    acc_ref[...] = jnp.zeros_like(acc_ref)

    def face_step(block, _):
        at = pl.ds(pl.multiple_of(block * CHUNK, CHUNK), CHUNK)
        cell = cell_ref[:, at]
        picked = dot(wide[...], as_bf16(one_hot(CX * CZ, cell // SP)))
        across = one_hot(SP, cell % SP)
        first = jnp.sum(jnp.where(across, picked[:128], 0.0), 0, keepdims=True)
        second = jnp.sum(jnp.where(across, picked[128:], 0.0), 0, keepdims=True)
        within = one_hot(64, rank_ref[:, at])
        stacked = jnp.concatenate(
            [jnp.where(within, first, 0.0).astype(bf16), jnp.where(within, second, 0.0).astype(bf16)], 0
        )
        acc_ref[...] += dot_nt(stacked, as_bf16(one_hot(256, owner_column(owner_ref[:, at]))))
        return 0

    lax.fori_loop(0, FACES // CHUNK, face_step, 0)
    pay_ref[...] = slots_from(acc_ref[0:64, :] + acc_ref[64:128, :]).reshape(GX, GZ, 128)


def fluid(flux, density, momentum, adjoint, objective, halos, owner, rank, cell):
    return pl.pallas_call(
        fluid_kernel,
        out_shape=(
            jax.ShapeDtypeStruct((5, CX, CZ, SP), f32),
            jax.ShapeDtypeStruct((CX * CZ, SP), f32),
            jax.ShapeDtypeStruct((GX, GZ, 128), f32),
        ),
        in_specs=[pl.BlockSpec(memory_space=pltpu.SMEM)] + [vmem()] * 12,
        out_specs=(vmem(),) * 3,
        scratch_shapes=[
            pltpu.VMEM((5, CX + 4, CZ, SP), f32),
            pltpu.VMEM((256, 512), bf16),
            pltpu.VMEM((128, 256), f32),
        ],
        compiler_params=pltpu.CompilerParams(vmem_limit_bytes=VMEM_LIMIT),
        name="fluid",
    )(flux, density, momentum, adjoint, objective, *halos, owner, rank, cell)


def shell_kernel(
    fixed_own, fixed_other, press_own, press_other, source, diag, coupling,
    shell_ref, answer_ref, fixed, press, rows_ref, table, acc_ref,
):
    col = lax.axis_index("col")
    half = lax.broadcasted_iota(i32, (GX, 4, 128), 2) // 64
    half_p = lax.broadcasted_iota(i32, (GX, 128), 1) // 64
    for g in range(GZ):
        other = fixed_other[g]
        fixed[g] = jnp.where(half == col, fixed_own[g], pltpu.roll(other, 64, 2))
        press[g] = jnp.where(half_p == col, press_own[g], pltpu.roll(press_other[g], 64, 1))
    acc_ref[...] = jnp.zeros_like(acc_ref)

    def row(g, k):
        return jnp.concatenate([fixed[g, x, k : k + 1, :] for x in range(GX)], 1)

    def add_step(g, _):
        node = row(g, 3).astype(i32)
        line = node // 128
        rows = as_bf16(one_hot(256, (line // 32) * 128 + node % 128))
        rows_ref[g] = rows
        columns = one_hot(32, line % 32)
        pressure = jnp.concatenate([press[g, x : x + 1, :] for x in range(GX)], 1)
        pieces = []
        for k in range(3):
            pieces += split(pressure * row(g, k))
        stacked = jnp.concatenate([jnp.where(columns, piece, 0.0).astype(bf16) for piece in pieces], 0)
        acc_ref[...] += dot_nt(stacked, rows)
        return 0

    lax.fori_loop(0, GZ, add_step, 0)
    loads = []
    for k in range(3):
        both = acc_ref[k * 64 : k * 64 + 32, :] + acc_ref[k * 64 + 32 : k * 64 + 64, :]
        loads.append(jnp.concatenate([both[:, :128], both[:, 128:]], 0) + source[:, k, :])
    for i in range(3):
        value = diag[:, i, :] * loads[i]
        for j in range(3):
            value = value + coupling[i, :, j, :] * loads[j]
        shell_ref[:, i, :] = value
        wide = jnp.concatenate([value[0:32], value[32:64]], 1)
        high, low = split(wide)
        table[i * 64 : i * 64 + 32, :] = high.astype(bf16)
        table[i * 64 + 32 : i * 64 + 64, :] = low.astype(bf16)

    def pick_step(g, _):
        picked = dot(table[...], rows_ref[g])
        node = row(g, 3).astype(i32)
        columns = one_hot(32, (node // 128) % 32)
        answer = jnp.zeros((1, GX * 128), f32)
        for k in range(3):
            both = picked[k * 64 : k * 64 + 32] + picked[k * 64 + 32 : k * 64 + 64]
            answer = answer + row(g, k) * jnp.sum(jnp.where(columns, both, 0.0), 0, keepdims=True)
        for x in range(GX):
            answer_ref[g, x : x + 1, :] = answer[:, x * 128 : x * 128 + 128]
        return 0

    lax.fori_loop(0, GZ, pick_step, 0)


def shell_part(fixed_own, fixed_other, press_own, press_other, source, diag, coupling):
    return pl.pallas_call(
        shell_kernel,
        out_shape=(
            jax.ShapeDtypeStruct((64, 3, 128), f32),
            jax.ShapeDtypeStruct((GZ, GX, 128), f32),
        ),
        in_specs=[vmem()] * 7,
        out_specs=(vmem(),) * 2,
        scratch_shapes=[
            pltpu.VMEM((GZ, GX, 4, 128), f32),
            pltpu.VMEM((GZ, GX, 128), f32),
            pltpu.VMEM((GZ, 256, GX * 128), bf16),
            pltpu.VMEM((192, 256), bf16),
            pltpu.VMEM((192, 256), f32),
        ],
        compiler_params=pltpu.CompilerParams(vmem_limit_bytes=VMEM_LIMIT),
        name="shell",
    )(fixed_own, fixed_other, press_own, press_other, source, diag, coupling)


def update_kernel(back, owner_ref, rank_ref, cell_ref, plane_ref, middle, out, wide, acc_ref, result, sem):
    turned = back[...].reshape(128, 128).T
    high, low = split(jnp.concatenate([turned[0:64], turned[64:128]], 1))
    wide[0:64, :] = high.astype(bf16)
    wide[64:128, :] = low.astype(bf16)
    acc_ref[...] = jnp.zeros_like(acc_ref)

    def face_step(block, _):
        at = pl.ds(pl.multiple_of(block * CHUNK, CHUNK), CHUNK)
        picked = dot(wide[...], as_bf16(one_hot(256, owner_column(owner_ref[:, at]))))
        within = one_hot(64, rank_ref[:, at])
        value = jnp.sum(jnp.where(within, picked[:64] + picked[64:], 0.0), 0, keepdims=True)
        first, second = split(value)
        cell = cell_ref[:, at]
        across = one_hot(SP, cell % SP)
        stacked = jnp.concatenate(
            [jnp.where(across, first, 0.0).astype(bf16), jnp.where(across, second, 0.0).astype(bf16)], 0
        )
        acc_ref[...] += dot_nt(as_bf16(one_hot(CX * CZ, cell // SP)), stacked)
        return 0

    lax.fori_loop(0, FACES // CHUNK, face_step, 0)
    result[...] = (plane_ref[...] + acc_ref[:, :128] + acc_ref[:, 128:]).reshape(CX, CZ, SP)
    copy = pltpu.make_async_copy(result, out.at[4], sem)
    copy.start()
    copy.wait()


def update(back, owner, rank, cell, plane, middle):
    return pl.pallas_call(
        update_kernel,
        out_shape=jax.ShapeDtypeStruct((5, CX, CZ, SP), f32),
        in_specs=[vmem()] * 5 + [pl.BlockSpec(memory_space=pl.ANY)],
        out_specs=pl.BlockSpec(memory_space=pl.ANY),
        input_output_aliases={5: 0},
        scratch_shapes=[
            pltpu.VMEM((128, 256), bf16),
            pltpu.VMEM((512, 256), f32),
            pltpu.VMEM((CX, CZ, SP), f32),
            pltpu.SemaphoreType.DMA,
        ],
        compiler_params=pltpu.CompilerParams(vmem_limit_bytes=VMEM_LIMIT),
        name="update",
    )(back, owner, rank, cell, plane, middle)


def body(
    density, momentum, adjoint, objective, flux_jac, wall_owner, wall_node, wall_cell,
    wall_weight, wall_normal, shell_source, shell_diag, shell_coupling,
):
    owner = wall_owner.reshape(1, FACES)
    node = wall_node.reshape(1, FACES)
    cell = wall_cell.reshape(1, FACES)
    weight = wall_weight.reshape(1, FACES)
    flux = flux_jac.reshape(75)
    source = shell_source.reshape(3, 64, 128).transpose(1, 0, 2)
    diag = shell_diag.reshape(3, 64, 128).transpose(1, 0, 2)
    coupling = shell_coupling.reshape(3, 3, 64, 128).transpose(0, 2, 1, 3)
    rank, pay = order(owner, node, weight, wall_normal)
    fixed_own, fixed_other, *halos = exchange_first(pay.reshape(4, GX, GZ, 128), adjoint)
    middle, plane, pay = fluid(flux, density, momentum, adjoint, objective, halos, owner, rank, cell)
    press_own, press_other = exchange_pressure(pay)
    shell, answers = shell_part(fixed_own, fixed_other, press_own, press_other, source, diag, coupling)
    back = exchange_back(answers)
    fluid_out = update(back, owner, rank, cell, plane, middle)
    return fluid_out, shell.transpose(1, 0, 2).reshape(3, NODES)


def solution(mesh):
    wall = ("gx", "gz", "col")
    return jax.shard_map(
        body,
        mesh=mesh,
        in_specs=(
            P(*wall),
            P(None, *wall),
            P(None, *wall),
            P(None, *wall),
            P(),
            P(wall, None),
            P(wall),
            P(wall),
            P(wall),
            P(None, wall),
            P(None, wall),
            P(None, wall),
            P(None, None, wall),
        ),
        out_specs=(P(None, *wall), P(None, wall)),
        check_vma=False,
    )
```

```python
import functools

import jax
import jax.numpy as jnp
from jax import lax
from jax.experimental import pallas as pl
from jax.experimental.pallas import tpu as pltpu
from jax.sharding import PartitionSpec as P

tau = 0.25
f32, bf16, i32 = jnp.float32, jnp.bfloat16, jnp.int32
MESH = pl.DeviceIdType.MESH
GX, GZ, COL = 8, 16, 2
CX, CZ, SP = 32, 16, 128
FACES, NODES = 8192, 8192
CHUNK = 2048
VMEM_LIMIT = 56 * 1024 * 1024


def vmem():
    return pl.BlockSpec(memory_space=pltpu.VMEM)


def split(x):
    high = x.astype(bf16).astype(f32)
    return high, x - high


def one_hot(rows, index):
    return lax.broadcasted_iota(i32, (rows, index.shape[1]), 0) == index


def as_bf16(mask):
    return jnp.where(mask, 1.0, 0.0).astype(bf16)


def dot(a, b):
    return jnp.dot(a, b, preferred_element_type=f32)


def dot_nt(a, b):
    return lax.dot_general(a, b, (((1,), (1,)), ((), ())), preferred_element_type=f32)


def owner_column(owner):
    return (owner % 2) * 128 + owner // 2


def slots_from(summed):
    return jnp.concatenate([summed[:, :128], summed[:, 128:]], 0).T


def place():
    return lax.axis_index("gx"), lax.axis_index("gz"), lax.axis_index("col")


def greet(gx, gz, col):
    barrier = pltpu.get_barrier_semaphore()
    for k in range(1, GX):
        pl.semaphore_signal(barrier, inc=1, device_id=((gx + k) % GX, gz, col), device_id_type=MESH)
    for k in range(1, GZ):
        pl.semaphore_signal(barrier, inc=1, device_id=(gx, (gz + k) % GZ, col), device_id_type=MESH)
    pl.semaphore_signal(barrier, inc=1, device_id=(gx, gz, 1 - col), device_id_type=MESH)


def greeted():
    pl.semaphore_wait(pltpu.get_barrier_semaphore(), GX + GZ - 1)


def remote(src, dst, sems, k, device):
    return pltpu.make_async_remote_copy(
        src_ref=src,
        dst_ref=dst,
        send_sem=sems.at[0, k],
        recv_sem=sems.at[1, k],
        device_id=device,
        device_id_type=MESH,
    )


class Stage:
    def __init__(self, copies, local=None):
        self.copies, self.local = copies, local

    def start(self):
        for copy in self.copies:
            copy.start()
        if self.local is not None:
            self.local.start()
        return self

    def arrive(self):
        for copy in self.copies:
            copy.wait_recv()
        if self.local is not None:
            self.local.wait()

    def sent(self):
        for copy in self.copies:
            copy.wait_send()


def along_gx(here, source, target, sems, local):
    gx, gz, col = here
    return Stage(
        [
            remote(source((gx + k) % GX), target(gx), sems, k - 1, ((gx + k) % GX, gz, col))
            for k in range(1, GX)
        ],
        pltpu.make_async_copy(source(gx), target(gx), local),
    )


def along_gz(here, source, target, sems, local):
    gx, gz, col = here
    return Stage(
        [
            remote(source((gz + k) % GZ), target(gz), sems, k - 1, (gx, (gz + k) % GZ, col))
            for k in range(1, GZ)
        ],
        pltpu.make_async_copy(source(gz), target(gz), local),
    )


def along_col(here, source, target, sems):
    gx, gz, col = here
    return Stage([remote(source, target, sems, 0, (gx, gz, 1 - col))])


def rank_faces(owner_ref, rank_ref, owners_ref, carry_ref):
    rows = lax.broadcasted_iota(i32, (256, 384), 0)
    cols = lax.broadcasted_iota(i32, (256, 384), 1)
    ahead = as_bf16((rows < cols) | (cols >= 256))
    carry_ref[...] = jnp.zeros_like(carry_ref)

    def step(block, _):
        at = pl.ds(pl.multiple_of(block * CHUNK, CHUNK), CHUNK)
        mask = one_hot(256, owner_column(owner_ref[:, at]))
        chosen = as_bf16(mask)
        owners_ref[:, at] = chosen
        carry = carry_ref[...]
        ranks = []
        for k in range(CHUNK // 256):
            counts = dot(chosen[:, k * 256 : k * 256 + 256], ahead)
            before = counts[:, :256] + jnp.concatenate([carry, carry], 1)
            ranks.append(
                jnp.sum(jnp.where(mask[:, k * 256 : k * 256 + 256], before, 0.0), 0, keepdims=True)
            )
            carry = carry + counts[:, 256:]
        rank_ref[:, at] = jnp.concatenate(ranks, 1).astype(i32)
        carry_ref[...] = carry
        return 0

    lax.fori_loop(0, FACES // CHUNK, step, 0)


def place_fixed(node_ref, weight_ref, normal_ref, rank_ref, owners_ref, acc_ref, pay):
    acc_ref[...] = jnp.zeros_like(acc_ref)

    def step(block, _):
        at = pl.ds(pl.multiple_of(block * CHUNK, CHUNK), CHUNK)
        within = one_hot(64, rank_ref[:, at])
        weight = weight_ref[:, at]
        node = node_ref[:, at]
        pieces = []
        for k in range(3):
            pieces += split(weight * normal_ref[k : k + 1, at])
        pieces += [((node // 128) * 128).astype(f32), (node % 128).astype(f32)]
        stacked = jnp.concatenate(
            [jnp.where(within, piece, 0.0).astype(bf16) for piece in pieces], 0
        )
        acc_ref[...] += dot_nt(stacked, owners_ref[:, at])
        return 0

    lax.fori_loop(0, FACES // CHUNK, step, 0)
    for k in range(4):
        pay[k] = slots_from(
            acc_ref[k * 128 : k * 128 + 64, :] + acc_ref[k * 128 + 64 : k * 128 + 128, :]
        ).reshape(GX, GZ, 128)


def stencil(here, flux, density, momentum, adjoint, objective, xlo, xhi, zlo, zhi, side, middle, plane_ref, ext):
    gx, gz, col = here
    lane = lax.broadcasted_iota(i32, (CZ, SP), 1)
    x_low = (gx > 0).astype(f32)
    x_high = (gx < GX - 1).astype(f32)
    z_low = (gz > 0).astype(f32)
    z_high = (gz < GZ - 1).astype(f32)
    s_low = (col > 0).astype(f32)
    s_high = (col < COL - 1).astype(f32)
    for j in range(5):
        ext[j, 0:2] = xlo[j] * x_low
        ext[j, CX + 2 : CX + 4] = xhi[j] * x_high

    def one_plane(x):
        inverse = (tau / 12.0) / density[x]
        velocity = [momentum[d, x] * inverse for d in range(3)]
        deltas = []
        for j in range(5):
            now = ext[j, x + 2]
            beside = side[j, x]
            dx = 8.0 * (ext[j, x + 1] - ext[j, x + 3]) - (ext[j, x] - ext[j, x + 4])
            tall = jnp.concatenate([zlo[j, x] * z_low, now, zhi[j, x] * z_high], 0)
            dz = 8.0 * (tall[1:17] - tall[3:19]) - (tall[0:16] - tall[4:20])
            low_side, high_side = beside * s_low, beside * s_high
            ds = 8.0 * (
                pltpu.roll(jnp.where(lane >= SP - 1, low_side, now), 1, 1)
                - pltpu.roll(jnp.where(lane < 1, high_side, now), SP - 1, 1)
            ) - (
                pltpu.roll(jnp.where(lane >= SP - 2, low_side, now), 2, 1)
                - pltpu.roll(jnp.where(lane < 2, high_side, now), SP - 2, 1)
            )
            deltas.append((dx, dz, ds))
        for i in range(5):
            total = velocity[0] * deltas[i][0] + velocity[1] * deltas[i][1] + velocity[2] * deltas[i][2]
            for d in range(3):
                for j in range(5):
                    total = total + (flux[j, d, i] * (tau / 12.0)) * deltas[j][d]
            value = ext[i, x + 2] - (total + tau * objective[i, x])
            middle[i, x] = value
            if i == 4:
                plane_ref[pl.ds(pl.multiple_of(x * CZ, CZ), CZ), :] = value

    def step(x, _):
        for k in range(2):
            one_plane(2 * x + k)
        return 0

    lax.fori_loop(0, CX // 2, step, 0)


def gather_pressure(cell_ref, rank_ref, owners_ref, plane_ref, wide, acc_ref, pay):
    high, low = split(plane_ref[...].T)
    wide[0:128, :] = high.astype(bf16)
    wide[128:256, :] = low.astype(bf16)
    acc_ref[0:128, :] = jnp.zeros((128, 256), f32)

    def step(block, _):
        at = pl.ds(pl.multiple_of(block * CHUNK, CHUNK), CHUNK)
        cell = cell_ref[:, at]
        picked = dot(wide[...], as_bf16(one_hot(CX * CZ, cell // SP)))
        across = one_hot(SP, cell % SP)
        first = jnp.sum(jnp.where(across, picked[:128], 0.0), 0, keepdims=True)
        second = jnp.sum(jnp.where(across, picked[128:], 0.0), 0, keepdims=True)
        within = one_hot(64, rank_ref[:, at])
        stacked = jnp.concatenate(
            [jnp.where(within, first, 0.0).astype(bf16), jnp.where(within, second, 0.0).astype(bf16)], 0
        )
        acc_ref[0:128, :] += dot_nt(stacked, owners_ref[:, at])
        return 0

    lax.fori_loop(0, FACES // CHUNK, step, 0)
    pay[...] = slots_from(acc_ref[0:64, :] + acc_ref[64:128, :]).reshape(GX, GZ, 128)


ROWS = GX * GZ * 128


def flat(ref, *tail):
    return lambda g: jnp.concatenate([ref[(g, slice(x, x + 1)) + tail] for x in range(GX)], 1)


def combine(col, own, other):
    half = lax.broadcasted_iota(i32, own.shape, own.ndim - 1) // 64
    return jnp.where(half == col, own, pltpu.roll(other, 64, own.ndim - 1))


def fixed_rows(col, own, other, fixed, rows_ref):
    for g in range(GZ):
        fixed[g] = combine(col, own[g], other[g])

    def step(g, _):
        for k in range(2):
            node = row(fixed, 2 * g + k, 3).astype(i32)
            line = node // 128
            rows_ref[2 * g + k] = as_bf16(one_hot(256, (line // 32) * 128 + node % 128))
        return 0

    lax.fori_loop(0, GZ // 2, step, 0)


def row(fixed, g, k):
    return jnp.concatenate([fixed[g, x, k : k + 1, :] for x in range(GX)], 1)


def node_columns(fixed, g):
    return one_hot(32, (row(fixed, g, 3).astype(i32) // 128) % 32)


def add_loads(press, fixed, rows_ref, acc_ref):
    acc_ref[0:192, :] = jnp.zeros((192, 256), f32)

    def step(h, _):
        total = acc_ref[0:192, :]
        for k in range(2):
            g = 2 * h + k
            columns = node_columns(fixed, g)
            pressure = jnp.concatenate([press[g, x : x + 1, :] for x in range(GX)], 1)
            pieces = []
            for c in range(3):
                pieces += split(pressure * row(fixed, g, c))
            stacked = jnp.concatenate([jnp.where(columns, piece, 0.0).astype(bf16) for piece in pieces], 0)
            total = total + dot_nt(stacked, rows_ref[g])
        acc_ref[0:192, :] = total
        return 0

    lax.fori_loop(0, GZ // 2, step, 0)


def solve_shell(acc_ref, source, diag, coupling, shell_ref, table):
    loads = []
    for k in range(3):
        both = acc_ref[k * 64 : k * 64 + 32, :] + acc_ref[k * 64 + 32 : k * 64 + 64, :]
        loads.append(jnp.concatenate([both[:, :128], both[:, 128:]], 0) + source[:, k, :])
    for i in range(3):
        value = diag[:, i, :] * loads[i]
        for j in range(3):
            value = value + coupling[i, :, j, :] * loads[j]
        shell_ref[:, i, :] = value
        wide = jnp.concatenate([value[0:32], value[32:64]], 1)
        high, low = split(wide)
        table[i * 64 : i * 64 + 32, :] = high.astype(bf16)
        table[i * 64 + 32 : i * 64 + 64, :] = low.astype(bf16)


def pick_answers(table, fixed, rows_ref, answers):
    def step(h, _):
        for k in range(2):
            g = 2 * h + k
            picked = dot(table[...], rows_ref[g])
            columns = node_columns(fixed, g)
            answer = jnp.zeros((1, GX * 128), f32)
            for c in range(3):
                both = picked[c * 64 : c * 64 + 32] + picked[c * 64 + 32 : c * 64 + 64]
                answer = answer + row(fixed, g, c) * jnp.sum(jnp.where(columns, both, 0.0), 0, keepdims=True)
            for x in range(GX):
                answers[g, x : x + 1, :] = answer[:, x * 128 : x * 128 + 128]
        return 0

    lax.fori_loop(0, GZ // 2, step, 0)


def main_kernel(
    owner, node, cell, weight, normal, source, diag, coupling,
    flux_hbm, density_hbm, momentum_hbm, adjoint_hbm, objective_hbm,
    rank, plane, shell, back, middle_hbm,
    flux, density, momentum, objective, ext, middle, xlo, xhi, zlo, zhi, side,
    owners, carry, acc, wide, rows_ref, table,
    pay0, hop0, own0, other0, fixed, pay1, hop1, own1, other1, press, answers, other2, mixed, hop2,
    sems_h, sems_z, sems_g, sems_c, local, loads,
):
    here = gx, gz, col = place()
    greet(gx, gz, col)
    staged = [
        pltpu.make_async_copy(adjoint_hbm, ext.at[:, 2 : CX + 2], loads.at[0]),
        pltpu.make_async_copy(momentum_hbm, momentum, loads.at[1]),
        pltpu.make_async_copy(density_hbm, density, loads.at[2]),
        pltpu.make_async_copy(objective_hbm, objective, loads.at[3]),
        pltpu.make_async_copy(flux_hbm, flux, loads.at[4]),
    ]
    for copy in staged:
        copy.start()
    rank_faces(owner, rank, owners, carry)
    greeted()
    up, down = ((gx + 1) % GX, gz, col), ((gx + GX - 1) % GX, gz, col)
    high, low = (gx, (gz + 1) % GZ, col), (gx, (gz + GZ - 1) % GZ, col)
    halos = Stage(
        [
            remote(adjoint_hbm.at[:, CX - 2 : CX], xlo, sems_h, 0, up),
            remote(adjoint_hbm.at[:, 0:2], xhi, sems_h, 1, down),
            remote(adjoint_hbm.at[:, :, CZ - 2 : CZ], zlo, sems_h, 2, high),
            remote(adjoint_hbm.at[:, :, 0:2], zhi, sems_h, 3, low),
            remote(adjoint_hbm, side, sems_h, 4, (gx, gz, 1 - col)),
        ]
    ).start()
    place_fixed(node, weight, normal, rank, owners, acc, pay0)
    fixed_z = along_gx(here, lambda x: pay0.at[:, x], lambda x: hop0.at[x], sems_z.at[0], local.at[0]).start()
    for copy in staged:
        copy.wait()
    halos.arrive()
    stencil(here, flux, density, momentum, adjoint_hbm, objective, xlo, xhi, zlo, zhi, side, middle, plane, ext)
    write = pltpu.make_async_copy(middle, middle_hbm, loads.at[5])
    write.start()
    fixed_z.arrive()
    fixed_g = along_gz(here, lambda z: hop0.at[:, :, z], lambda z: own0.at[z], sems_g.at[0], local.at[1]).start()
    gather_pressure(cell, rank, owners, plane, wide, acc, pay1)
    press_z = along_gx(here, lambda x: pay1.at[x], lambda x: hop1.at[x], sems_z.at[1], local.at[2]).start()
    fixed_g.arrive()
    fixed_c = along_col(here, own0, other0, sems_c.at[0]).start()
    press_z.arrive()
    press_g = along_gz(here, lambda z: hop1.at[:, z], lambda z: own1.at[z], sems_g.at[1], local.at[3]).start()
    fixed_c.arrive()
    fixed_rows(col, own0, other0, fixed, rows_ref)
    press_g.arrive()
    press_c = along_col(here, own1, other1, sems_c.at[1]).start()
    press_c.arrive()
    for g in range(GZ):
        press[g] = combine(col, own1[g], other1[g])
    add_loads(press, fixed, rows_ref, acc)
    solve_shell(acc, source, diag, coupling, shell, table)
    pick_answers(table, fixed, rows_ref, answers)
    back_c = along_col(here, answers, other2, sems_c.at[2]).start()
    back_c.arrive()
    for g in range(GZ):
        mixed[g] = combine(col, answers[g], other2[g])
    back_g = along_gz(here, lambda z: mixed.at[z], lambda z: hop2.at[:, z], sems_g.at[2], local.at[4]).start()
    back_g.arrive()
    back_z = along_gx(here, lambda x: hop2.at[x], lambda x: back.at[x], sems_z.at[2], local.at[5]).start()
    back_z.arrive()
    write.wait()
    for stage in (halos, fixed_z, fixed_g, fixed_c, press_z, press_g, press_c, back_c, back_g, back_z):
        stage.sent()


def main_part(owner, node, cell, weight, normal, source, diag, coupling, flux, density, momentum, adjoint, objective):
    hbm = pl.BlockSpec(memory_space=pl.ANY)
    dma = pltpu.SemaphoreType.DMA
    block = (5, CX, CZ, SP)
    return pl.pallas_call(
        main_kernel,
        out_shape=(
            jax.ShapeDtypeStruct((1, FACES), i32),
            jax.ShapeDtypeStruct((CX * CZ, SP), f32),
            jax.ShapeDtypeStruct((64, 3, 128), f32),
            jax.ShapeDtypeStruct((GX, GZ, 128), f32),
            jax.ShapeDtypeStruct(block, f32),
        ),
        in_specs=[vmem()] * 8 + [hbm] * 5,
        out_specs=(vmem(),) * 4 + (hbm,),
        scratch_shapes=[
            pltpu.SMEM((5, 3, 5), f32),
            pltpu.VMEM((CX, CZ, SP), f32),
            pltpu.VMEM((3, CX, CZ, SP), f32),
            pltpu.VMEM(block, f32),
            pltpu.VMEM((5, CX + 4, CZ, SP), f32),
            pltpu.VMEM(block, f32),
            pltpu.VMEM((5, 2, CZ, SP), f32),
            pltpu.VMEM((5, 2, CZ, SP), f32),
            pltpu.VMEM((5, CX, 2, SP), f32),
            pltpu.VMEM((5, CX, 2, SP), f32),
            pltpu.VMEM(block, f32),
            pltpu.VMEM((256, FACES), bf16),
            pltpu.VMEM((256, 128), f32),
            pltpu.VMEM((512, 256), f32),
            pltpu.VMEM((256, 512), bf16),
            pltpu.VMEM((GZ, 256, GX * 128), bf16),
            pltpu.VMEM((192, 256), bf16),
            pltpu.VMEM((4, GX, GZ, 128), f32),
            pltpu.VMEM((GX, 4, GZ, 128), f32),
            pltpu.VMEM((GZ, GX, 4, 128), f32),
            pltpu.VMEM((GZ, GX, 4, 128), f32),
            pltpu.VMEM((GZ, GX, 4, 128), f32),
            pltpu.VMEM((GX, GZ, 128), f32),
            pltpu.VMEM((GX, GZ, 128), f32),
            pltpu.VMEM((GZ, GX, 128), f32),
            pltpu.VMEM((GZ, GX, 128), f32),
            pltpu.VMEM((GZ, GX, 128), f32),
            pltpu.VMEM((GZ, GX, 128), f32),
            pltpu.VMEM((GZ, GX, 128), f32),
            pltpu.VMEM((GZ, GX, 128), f32),
            pltpu.VMEM((GX, GZ, 128), f32),
            dma((2, 5)),
            dma((3, 2, GX - 1)),
            dma((3, 2, GZ - 1)),
            dma((3, 2, 1)),
            dma((6,)),
            dma((6,)),
        ],
        compiler_params=pltpu.CompilerParams(
            collective_id=0, has_side_effects=True, vmem_limit_bytes=VMEM_LIMIT
        ),
        name="main",
    )(owner, node, cell, weight, normal, source, diag, coupling, flux, density, momentum, adjoint, objective)


def update_kernel(
    back, owner_ref, rank_ref, cell_ref, plane_ref, middle, shell, out, shell_out, wide, acc_ref, result, passing, nodes, sems
):
    taken = [
        pltpu.make_async_copy(middle.at[0:4], passing, sems.at[0]),
        pltpu.make_async_copy(shell, nodes, sems.at[1]),
    ]
    given = [
        pltpu.make_async_copy(passing, out.at[0:4], sems.at[2]),
        pltpu.make_async_copy(nodes, shell_out, sems.at[3]),
        pltpu.make_async_copy(result, out.at[4], sems.at[4]),
    ]
    for copy in taken:
        copy.start()
    turned = back[...].reshape(128, 128).T
    high, low = split(jnp.concatenate([turned[0:64], turned[64:128]], 1))
    wide[0:64, :] = high.astype(bf16)
    wide[64:128, :] = low.astype(bf16)
    acc_ref[...] = jnp.zeros_like(acc_ref)

    def face_step(block, _):
        @pl.when(block == 1)
        def _():
            for k in range(2):
                taken[k].wait()
                given[k].start()

        at = pl.ds(pl.multiple_of(block * CHUNK, CHUNK), CHUNK)
        picked = dot(wide[...], as_bf16(one_hot(256, owner_column(owner_ref[:, at]))))
        within = one_hot(64, rank_ref[:, at])
        value = jnp.sum(jnp.where(within, picked[:64] + picked[64:], 0.0), 0, keepdims=True)
        first, second = split(value)
        cell = cell_ref[:, at]
        across = one_hot(SP, cell % SP)
        stacked = jnp.concatenate(
            [jnp.where(across, first, 0.0).astype(bf16), jnp.where(across, second, 0.0).astype(bf16)], 0
        )
        acc_ref[...] += dot_nt(as_bf16(one_hot(CX * CZ, cell // SP)), stacked)
        return 0

    lax.fori_loop(0, FACES // CHUNK, face_step, 0)
    result[...] = (plane_ref[...] + acc_ref[:, :128] + acc_ref[:, 128:]).reshape(CX, CZ, SP)
    given[2].start()
    for copy in given:
        copy.wait()


def update(back, owner, rank, cell, plane, middle, shell):
    hbm = pl.BlockSpec(memory_space=pl.ANY)
    return pl.pallas_call(
        update_kernel,
        out_shape=(
            jax.ShapeDtypeStruct((5, CX, CZ, SP), f32),
            jax.ShapeDtypeStruct((64, 3, 128), f32),
        ),
        in_specs=[vmem()] * 5 + [hbm] * 2,
        out_specs=(hbm, hbm),
        scratch_shapes=[
            pltpu.VMEM((128, 256), bf16),
            pltpu.VMEM((512, 256), f32),
            pltpu.VMEM((CX, CZ, SP), f32),
            pltpu.VMEM((4, CX, CZ, SP), f32),
            pltpu.VMEM((64, 3, 128), f32),
            pltpu.SemaphoreType.DMA((5,)),
        ],
        compiler_params=pltpu.CompilerParams(vmem_limit_bytes=VMEM_LIMIT),
        name="update",
    )(back, owner, rank, cell, plane, middle, shell)


def body(
    density, momentum, adjoint, objective, flux_jac, wall_owner, wall_node, wall_cell,
    wall_weight, wall_normal, shell_source, shell_diag, shell_coupling,
):
    owner = wall_owner.reshape(1, FACES)
    node = wall_node.reshape(1, FACES)
    cell = wall_cell.reshape(1, FACES)
    weight = wall_weight.reshape(1, FACES)
    source = shell_source.reshape(3, 64, 128).transpose(1, 0, 2)
    diag = shell_diag.reshape(3, 64, 128).transpose(1, 0, 2)
    coupling = shell_coupling.reshape(3, 3, 64, 128).transpose(0, 2, 1, 3)
    rank, plane, shell, back, middle = main_part(
        owner, node, cell, weight, wall_normal, source, diag, coupling,
        flux_jac.transpose(1, 0, 2), density, momentum, adjoint, objective,
    )
    fluid_out, shell = update(back, owner, rank, cell, plane, middle, shell)
    return fluid_out, shell.transpose(1, 0, 2).reshape(3, NODES)


def solution(mesh):
    wall = ("gx", "gz", "col")
    return jax.shard_map(
        body,
        mesh=mesh,
        in_specs=(
            P(*wall),
            P(None, *wall),
            P(None, *wall),
            P(None, *wall),
            P(),
            P(wall, None),
            P(wall),
            P(wall),
            P(wall),
            P(None, wall),
            P(None, wall),
            P(None, wall),
            P(None, None, wall),
        ),
        out_specs=(P(None, *wall), P(None, wall)),
        check_vma=False,
    )
```

```python
import functools

import jax
import jax.numpy as jnp
from jax import lax
from jax.experimental import pallas as pl
from jax.experimental.pallas import tpu as pltpu
from jax.sharding import PartitionSpec as P

tau = 0.25
f32, bf16, i32 = jnp.float32, jnp.bfloat16, jnp.int32
MESH = pl.DeviceIdType.MESH
GX, GZ, COL = 8, 16, 2
CX, CZ, SP = 32, 16, 128
FACES, NODES = 8192, 8192
ZB = 8
CHUNK = 2048
VMEM_LIMIT = 56 * 1024 * 1024


def vmem():
    return pl.BlockSpec(memory_space=pltpu.VMEM)


def split(x):
    high = x.astype(bf16).astype(f32)
    return high, x - high


def one_hot(rows, index):
    return lax.broadcasted_iota(i32, (rows, index.shape[1]), 0) == index


def as_bf16(mask):
    return jnp.where(mask, 1.0, 0.0).astype(bf16)


def dot(a, b):
    return jnp.dot(a, b, preferred_element_type=f32)


def dot_nt(a, b):
    return lax.dot_general(a, b, (((1,), (1,)), ((), ())), preferred_element_type=f32)


def owner_column(owner):
    return (owner % 2) * 128 + owner // 2


def slots_from(summed):
    return jnp.concatenate([summed[:, :128], summed[:, 128:]], 0).T


def place():
    return lax.axis_index("gx"), lax.axis_index("gz"), lax.axis_index("col")


def greet(gx, gz, col):
    barrier = pltpu.get_barrier_semaphore()
    for k in range(1, GX):
        pl.semaphore_signal(barrier, inc=1, device_id=((gx + k) % GX, gz, col), device_id_type=MESH)
    for k in range(1, GZ):
        pl.semaphore_signal(barrier, inc=1, device_id=(gx, (gz + k) % GZ, col), device_id_type=MESH)
    pl.semaphore_signal(barrier, inc=1, device_id=(gx, gz, 1 - col), device_id_type=MESH)


def greeted():
    pl.semaphore_wait(pltpu.get_barrier_semaphore(), GX + GZ - 1)


def remote(src, dst, sems, k, device):
    return pltpu.make_async_remote_copy(
        src_ref=src,
        dst_ref=dst,
        send_sem=sems.at[0, k],
        recv_sem=sems.at[1, k],
        device_id=device,
        device_id_type=MESH,
    )


class Stage:
    def __init__(self, copies, local=None):
        self.copies, self.local = copies, local

    def start(self):
        for copy in self.copies:
            copy.start()
        if self.local is not None:
            self.local.start()
        return self

    def arrive(self):
        for copy in self.copies:
            copy.wait_recv()
        if self.local is not None:
            self.local.wait()

    def sent(self):
        for copy in self.copies:
            copy.wait_send()


def along_gx(here, source, target, sems, local):
    gx, gz, col = here
    return Stage(
        [
            remote(source((gx + k) % GX), target(gx), sems, k - 1, ((gx + k) % GX, gz, col))
            for k in range(1, GX)
        ],
        pltpu.make_async_copy(source(gx), target(gx), local),
    )


def along_gz(here, source, target, sems, local):
    gx, gz, col = here
    return Stage(
        [
            remote(source((gz + k) % GZ), target(gz), sems, k - 1, (gx, (gz + k) % GZ, col))
            for k in range(1, GZ)
        ],
        pltpu.make_async_copy(source(gz), target(gz), local),
    )


def along_col(here, source, target, sems):
    gx, gz, col = here
    return Stage([remote(source, target, sems, 0, (gx, gz, 1 - col))])


def rank_faces(owner_ref, rank_ref, owners_ref, carry_ref):
    rows = lax.broadcasted_iota(i32, (256, 384), 0)
    cols = lax.broadcasted_iota(i32, (256, 384), 1)
    ahead = as_bf16((rows < cols) | (cols >= 256))
    carry_ref[...] = jnp.zeros_like(carry_ref)

    def step(block, _):
        at = pl.ds(pl.multiple_of(block * CHUNK, CHUNK), CHUNK)
        mask = one_hot(256, owner_column(owner_ref[:, at]))
        chosen = as_bf16(mask)
        owners_ref[:, at] = chosen
        carry = carry_ref[...]
        ranks = []
        for k in range(CHUNK // 256):
            counts = dot(chosen[:, k * 256 : k * 256 + 256], ahead)
            before = counts[:, :256] + jnp.concatenate([carry, carry], 1)
            ranks.append(
                jnp.sum(jnp.where(mask[:, k * 256 : k * 256 + 256], before, 0.0), 0, keepdims=True)
            )
            carry = carry + counts[:, 256:]
        rank_ref[:, at] = jnp.concatenate(ranks, 1).astype(i32)
        carry_ref[...] = carry
        return 0

    lax.fori_loop(0, FACES // CHUNK, step, 0)


def place_fixed(first, last, node_ref, weight_ref, normal_ref, rank_ref, owners_ref, acc_ref):
    if first == 0:
        acc_ref[...] = jnp.zeros_like(acc_ref)

    def step(block, _):
        at = pl.ds(pl.multiple_of(block * CHUNK, CHUNK), CHUNK)
        within = one_hot(64, rank_ref[:, at])
        weight = weight_ref[:, at]
        node = node_ref[:, at]
        pieces = []
        for k in range(3):
            pieces += split(weight * normal_ref[k : k + 1, at])
        pieces += [((node // 128) * 128).astype(f32), (node % 128).astype(f32)]
        stacked = jnp.concatenate(
            [jnp.where(within, piece, 0.0).astype(bf16) for piece in pieces], 0
        )
        acc_ref[...] += dot_nt(stacked, owners_ref[:, at])
        return 0

    lax.fori_loop(first, last, step, 0)


def fixed_payload(acc_ref, pay):
    for k in range(4):
        pay[k] = slots_from(
            acc_ref[k * 128 : k * 128 + 64, :] + acc_ref[k * 128 + 64 : k * 128 + 128, :]
        ).reshape(GX, GZ, 128)


def pack_side(col, ext, packed):
    lane = lax.broadcasted_iota(i32, (CZ, SP), 1)
    shift = 2 * (1 - col)

    def step(block, kept):
        kept = list(kept)
        for k in range(4):
            x = block * 4 + k
            here = (lane // 2) == x
            for j in range(5):
                kept[j] = jnp.where(here, pltpu.roll(ext[j, x + 2, ZB : ZB + CZ], 2 * x + shift, 1), kept[j])
        return tuple(kept)

    kept = lax.fori_loop(0, CX // 4, step, (jnp.zeros((CZ, SP), f32),) * 5)
    for j in range(5):
        packed[j] = kept[j]


def stencil(here, flux, density, momentum, objective, side, middle, plane_ref, ext):
    gx, gz, col = here
    lane = lax.broadcasted_iota(i32, (CZ, SP), 1)
    s_low = (col > 0).astype(f32)
    s_high = (col < COL - 1).astype(f32)
    inner = slice(ZB, ZB + CZ)
    nothing = functools.partial(jnp.zeros, dtype=f32)

    @pl.when(gx == 0)
    def _():
        ext[:, 0:2, inner] = nothing((5, 2, CZ, SP))

    @pl.when(gx == GX - 1)
    def _():
        ext[:, CX + 2 : CX + 4, inner] = nothing((5, 2, CZ, SP))

    @pl.when(gz == 0)
    def _():
        ext[:, 2 : CX + 2, ZB - 2 : ZB] = nothing((5, CX, 2, SP))

    @pl.when(gz == GZ - 1)
    def _():
        ext[:, 2 : CX + 2, ZB + CZ : ZB + CZ + 2] = nothing((5, CX, 2, SP))

    def one_plane(x):
        unpack = (2 * SP + 126 * col - 2 * x) % SP
        inverse = (tau / 12.0) / density[x]
        velocity = [momentum[d, x] * inverse for d in range(3)]
        deltas = []
        for j in range(5):
            now = ext[j, x + 2, inner]
            beside = pltpu.roll(side[j], unpack, 1)
            dx = 8.0 * (ext[j, x + 1, inner] - ext[j, x + 3, inner]) - (ext[j, x, inner] - ext[j, x + 4, inner])
            near = ext[j, x + 2, ZB - 1 : ZB - 1 + CZ] - ext[j, x + 2, ZB + 1 : ZB + 1 + CZ]
            far = ext[j, x + 2, ZB - 2 : ZB - 2 + CZ] - ext[j, x + 2, ZB + 2 : ZB + 2 + CZ]
            dz = 8.0 * near - far
            low_side, high_side = beside * s_low, beside * s_high
            ds = 8.0 * (
                pltpu.roll(jnp.where(lane >= SP - 1, low_side, now), 1, 1)
                - pltpu.roll(jnp.where(lane < 1, high_side, now), SP - 1, 1)
            ) - (
                pltpu.roll(jnp.where(lane >= SP - 2, low_side, now), 2, 1)
                - pltpu.roll(jnp.where(lane < 2, high_side, now), SP - 2, 1)
            )
            deltas.append((dx, dz, ds))
        for i in range(5):
            total = velocity[0] * deltas[i][0] + velocity[1] * deltas[i][1] + velocity[2] * deltas[i][2]
            for d in range(3):
                for j in range(5):
                    total = total + (flux[j, d, i] * (tau / 12.0)) * deltas[j][d]
            value = ext[i, x + 2, inner] - (total + tau * objective[i, x])
            middle[i, x] = value
            if i == 4:
                plane_ref[pl.ds(pl.multiple_of(x * CZ, CZ), CZ), :] = value

    def step(x, _):
        for k in range(2):
            one_plane(2 * x + k)
        return 0

    lax.fori_loop(0, CX // 2, step, 0)


def cell_rows(cell_ref, cells_ref):
    def step(block, _):
        at = pl.ds(pl.multiple_of(block * CHUNK, CHUNK), CHUNK)
        cells_ref[:, at] = as_bf16(one_hot(CX * CZ, cell_ref[:, at] // SP))
        return 0

    lax.fori_loop(0, FACES // CHUNK, step, 0)


def split_plane(plane_ref, wide, acc_ref):
    high, low = split(plane_ref[...].T)
    wide[0:128, :] = high.astype(bf16)
    wide[128:256, :] = low.astype(bf16)
    acc_ref[0:128, :] = jnp.zeros((128, 256), f32)


def gather_pressure(first, last, cell_ref, cells_ref, rank_ref, owners_ref, wide, acc_ref):
    def step(block, _):
        at = pl.ds(pl.multiple_of(block * CHUNK, CHUNK), CHUNK)
        picked = dot(wide[...], cells_ref[:, at])
        across = one_hot(SP, cell_ref[:, at] % SP)
        high = jnp.sum(jnp.where(across, picked[:128], 0.0), 0, keepdims=True)
        low = jnp.sum(jnp.where(across, picked[128:], 0.0), 0, keepdims=True)
        within = one_hot(64, rank_ref[:, at])
        stacked = jnp.concatenate(
            [jnp.where(within, high, 0.0).astype(bf16), jnp.where(within, low, 0.0).astype(bf16)], 0
        )
        acc_ref[0:128, :] += dot_nt(stacked, owners_ref[:, at])
        return 0

    lax.fori_loop(first, last, step, 0)


def pressure_payload(acc_ref, pay):
    pay[...] = slots_from(acc_ref[0:64, :] + acc_ref[64:128, :]).reshape(GX, GZ, 128)


WAYS = 4


def combine(col, own, other):
    half = lax.broadcasted_iota(i32, own.shape, own.ndim - 1) // 64
    return jnp.where(half == col, own, pltpu.roll(other, 64, own.ndim - 1))


def compact(col, rows, target, first):
    for h in range(GZ // 2):
        target[first + h] = combine(col, rows[2 * h + col], rows[2 * h + 1 - col])


def fixed_rows(first, last, fixed, rows_ref):
    def step(h, _):
        for k in range(WAYS):
            g = WAYS * h + k
            node = row(fixed, g, 3).astype(i32)
            line = node // 128
            rows_ref[g] = as_bf16(one_hot(256, (line // 32) * 128 + node % 128))
        return 0

    lax.fori_loop(first, last, step, 0)


def row(fixed, g, k):
    return jnp.concatenate([fixed[g, x, k : k + 1, :] for x in range(GX)], 1)


def node_columns(fixed, g):
    return one_hot(32, (row(fixed, g, 3).astype(i32) // 128) % 32)


def add_loads(first, last, press, fixed, rows_ref, acc_ref):
    if first == 0:
        acc_ref[0:192, :] = jnp.zeros((192, 256), f32)

    def step(h, _):
        total = acc_ref[0:192, :]
        for k in range(WAYS):
            g = WAYS * h + k
            columns = node_columns(fixed, g)
            pressure = jnp.concatenate([press[g, x : x + 1, :] for x in range(GX)], 1)
            pieces = []
            for c in range(3):
                pieces += split(pressure * row(fixed, g, c))
            stacked = jnp.concatenate([jnp.where(columns, piece, 0.0).astype(bf16) for piece in pieces], 0)
            total = total + dot_nt(stacked, rows_ref[g])
        acc_ref[0:192, :] = total
        return 0

    lax.fori_loop(first, last, step, 0)


def solve_shell(acc_ref, source, diag, coupling, shell_ref, table):
    loads = []
    for k in range(3):
        both = acc_ref[k * 64 : k * 64 + 32, :] + acc_ref[k * 64 + 32 : k * 64 + 64, :]
        loads.append(jnp.concatenate([both[:, :128], both[:, 128:]], 0) + source[:, k, :])
    for i in range(3):
        value = diag[:, i, :] * loads[i]
        for j in range(3):
            value = value + coupling[i, :, j, :] * loads[j]
        shell_ref[:, i, :] = value
        wide = jnp.concatenate([value[0:32], value[32:64]], 1)
        high, low = split(wide)
        table[i * 64 : i * 64 + 32, :] = high.astype(bf16)
        table[i * 64 + 32 : i * 64 + 64, :] = low.astype(bf16)


def pick_answers(first, last, table, fixed, rows_ref, answers):
    def step(h, _):
        for k in range(WAYS):
            g = WAYS * h + k
            picked = dot(table[...], rows_ref[g])
            columns = node_columns(fixed, g)
            answer = jnp.zeros((1, GX * 128), f32)
            for c in range(3):
                both = picked[c * 64 : c * 64 + 32] + picked[c * 64 + 32 : c * 64 + 64]
                answer = answer + row(fixed, g, c) * jnp.sum(jnp.where(columns, both, 0.0), 0, keepdims=True)
            for x in range(GX):
                answers[g, x : x + 1, :] = answer[:, x * 128 : x * 128 + 128]
        return 0

    lax.fori_loop(first, last, step, 0)


def mix_answers(col, answers, other, mixed):
    for h in range(GZ // 2):
        mixed[2 * h + col] = combine(col, answers[h], other[h])
        mixed[2 * h + 1 - col] = combine(1 - col, other[h], answers[h])


def main_kernel(
    owner, node_hbm, cell_hbm, weight_hbm, normal_hbm, source_hbm, diag_hbm, coupling_hbm,
    flux_hbm, density_hbm, momentum_hbm, adjoint_hbm, objective_hbm,
    back, rank_hbm, plane_hbm, shell_hbm, middle_hbm,
    node, cell, weight, normal, source, diag, coupling, rank, plane, shell,
    flux, density, momentum, objective, ext, middle, packed, side,
    owners, cells, carry, acc, wide, rows_ref, table,
    pay0, hop0, own0, other0, fixed, pay1, hop1, own1, other1, press, answers, other2, mixed, hop2,
    sems_h, sems_z, sems_g, sems_c, local, loads, stores,
):
    here = gx, gz, col = place()
    greet(gx, gz, col)
    staged = [
        pltpu.make_async_copy(source_ref, target, loads.at[k])
        for k, (source_ref, target) in enumerate(
            [
                (adjoint_hbm, ext.at[:, 2 : CX + 2, ZB : ZB + CZ]),
                (node_hbm, node),
                (weight_hbm, weight),
                (normal_hbm, normal),
                (cell_hbm, cell),
                (flux_hbm, flux),
                (density_hbm, density),
                (momentum_hbm, momentum),
                (objective_hbm, objective),
                (source_hbm, source),
                (diag_hbm, diag),
                (coupling_hbm, coupling),
            ]
        )
    ]
    for copy in staged:
        copy.start()
    rank_faces(owner, rank, owners, carry)
    staged[0].wait()
    pack_side(col, ext, packed)
    greeted()
    up, down = ((gx + 1) % GX, gz, col), ((gx + GX - 1) % GX, gz, col)
    high, low = (gx, (gz + 1) % GZ, col), (gx, (gz + GZ - 1) % GZ, col)
    planes, inner = slice(2, CX + 2), slice(ZB, ZB + CZ)
    halos = Stage(
        [
            remote(ext.at[:, planes, ZB + CZ - 2 : ZB + CZ], ext.at[:, planes, ZB - 2 : ZB], sems_h, 2, high),
            remote(ext.at[:, planes, ZB : ZB + 2], ext.at[:, planes, ZB + CZ : ZB + CZ + 2], sems_h, 3, low),
            remote(ext.at[:, CX : CX + 2, inner], ext.at[:, 0:2, inner], sems_h, 0, up),
            remote(ext.at[:, 2:4, inner], ext.at[:, CX + 2 : CX + 4, inner], sems_h, 1, down),
            remote(packed, side, sems_h, 4, (gx, gz, 1 - col)),
        ]
    ).start()
    for copy in staged[1:]:
        copy.wait()
    place_fixed(0, 4, node, weight, normal, rank, owners, acc)
    fixed_payload(acc, pay0)
    fixed_z = along_gx(here, lambda x: pay0.at[:, x], lambda x: hop0.at[x], sems_z.at[0], local.at[0]).start()
    cell_rows(cell, cells)
    halos.arrive()
    stencil(here, flux, density, momentum, objective, side, middle, plane, ext)
    written = [
        pltpu.make_async_copy(middle, middle_hbm, stores.at[0]),
        pltpu.make_async_copy(plane, plane_hbm, stores.at[1]),
        pltpu.make_async_copy(rank, rank_hbm, stores.at[2]),
    ]
    for copy in written:
        copy.start()
    split_plane(plane, wide, acc)
    gather_pressure(0, 3, cell, cells, rank, owners, wide, acc)
    fixed_z.arrive()
    fixed_g = along_gz(here, lambda z: hop0.at[:, :, z], lambda z: own0.at[z], sems_g.at[0], local.at[1]).start()
    gather_pressure(3, 4, cell, cells, rank, owners, wide, acc)
    pressure_payload(acc, pay1)
    press_z = along_gx(here, lambda x: pay1.at[x], lambda x: hop1.at[x], sems_z.at[1], local.at[2]).start()
    press_z.arrive()
    press_g = along_gz(here, lambda z: hop1.at[:, z], lambda z: own1.at[z], sems_g.at[1], local.at[3]).start()
    half = GZ // WAYS // 2
    fixed_g.arrive()
    fixed_c = along_col(here, own0, other0, sems_c.at[0]).start()
    compact(col, own0, fixed, 0)
    fixed_rows(0, half, fixed, rows_ref)
    fixed_c.arrive()
    compact(col, other0, fixed, GZ // 2)
    fixed_rows(half, 2 * half, fixed, rows_ref)
    press_g.arrive()
    press_c = along_col(here, own1, other1, sems_c.at[1]).start()
    compact(col, own1, press, 0)
    add_loads(0, half, press, fixed, rows_ref, acc)
    press_c.arrive()
    compact(col, other1, press, GZ // 2)
    add_loads(half, 2 * half, press, fixed, rows_ref, acc)
    solve_shell(acc, source, diag, coupling, shell, table)
    written.append(pltpu.make_async_copy(shell, shell_hbm, stores.at[3]))
    written[3].start()
    pick_answers(half, 2 * half, table, fixed, rows_ref, answers)
    back_c = along_col(here, answers.at[GZ // 2 : GZ], other2, sems_c.at[2]).start()
    pick_answers(0, half, table, fixed, rows_ref, answers)
    back_c.arrive()
    mix_answers(col, answers, other2, mixed)
    back_g = along_gz(here, lambda z: mixed.at[z], lambda z: hop2.at[:, z], sems_g.at[2], local.at[4]).start()
    back_g.arrive()
    back_z = along_gx(here, lambda x: hop2.at[x], lambda x: back.at[x], sems_z.at[2], local.at[5]).start()
    back_z.arrive()
    for copy in written:
        copy.wait()
    for stage in (halos, fixed_z, fixed_g, fixed_c, press_z, press_g, press_c, back_c, back_g, back_z):
        stage.sent()


def main_part(owner, node, cell, weight, normal, source, diag, coupling, flux, density, momentum, adjoint, objective):
    hbm = pl.BlockSpec(memory_space=pl.ANY)
    dma = pltpu.SemaphoreType.DMA
    block = (5, CX, CZ, SP)
    return pl.pallas_call(
        main_kernel,
        out_shape=(
            jax.ShapeDtypeStruct((GX, GZ, 128), f32),
            jax.ShapeDtypeStruct((1, FACES), i32),
            jax.ShapeDtypeStruct((CX * CZ, SP), f32),
            jax.ShapeDtypeStruct((64, 3, 128), f32),
            jax.ShapeDtypeStruct(block, f32),
        ),
        in_specs=[vmem()] + [hbm] * 12,
        out_specs=(vmem(),) + (hbm,) * 4,
        scratch_shapes=[
            pltpu.VMEM((1, FACES), i32),
            pltpu.VMEM((1, FACES), i32),
            pltpu.VMEM((1, FACES), f32),
            pltpu.VMEM((3, FACES), f32),
            pltpu.VMEM((64, 3, 128), f32),
            pltpu.VMEM((64, 3, 128), f32),
            pltpu.VMEM((3, 64, 3, 128), f32),
            pltpu.VMEM((1, FACES), i32),
            pltpu.VMEM((CX * CZ, SP), f32),
            pltpu.VMEM((64, 3, 128), f32),
            pltpu.SMEM((5, 3, 5), f32),
            pltpu.VMEM((CX, CZ, SP), f32),
            pltpu.VMEM((3, CX, CZ, SP), f32),
            pltpu.VMEM(block, f32),
            pltpu.VMEM((5, CX + 4, 2 * ZB + CZ, SP), f32),
            pltpu.VMEM(block, f32),
            pltpu.VMEM((5, CZ, SP), f32),
            pltpu.VMEM((5, CZ, SP), f32),
            pltpu.VMEM((256, FACES), bf16),
            pltpu.VMEM((CX * CZ, FACES), bf16),
            pltpu.VMEM((256, 128), f32),
            pltpu.VMEM((512, 256), f32),
            pltpu.VMEM((256, 512), bf16),
            pltpu.VMEM((GZ, 256, GX * 128), bf16),
            pltpu.VMEM((192, 256), bf16),
            pltpu.VMEM((4, GX, GZ, 128), f32),
            pltpu.VMEM((GX, 4, GZ, 128), f32),
            pltpu.VMEM((GZ, GX, 4, 128), f32),
            pltpu.VMEM((GZ, GX, 4, 128), f32),
            pltpu.VMEM((GZ, GX, 4, 128), f32),
            pltpu.VMEM((GX, GZ, 128), f32),
            pltpu.VMEM((GX, GZ, 128), f32),
            pltpu.VMEM((GZ, GX, 128), f32),
            pltpu.VMEM((GZ, GX, 128), f32),
            pltpu.VMEM((GZ, GX, 128), f32),
            pltpu.VMEM((GZ, GX, 128), f32),
            pltpu.VMEM((GZ // 2, GX, 128), f32),
            pltpu.VMEM((GZ, GX, 128), f32),
            pltpu.VMEM((GX, GZ, 128), f32),
            dma((2, 5)),
            dma((3, 2, GX - 1)),
            dma((3, 2, GZ - 1)),
            dma((3, 2, 1)),
            dma((6,)),
            dma((12,)),
            dma((4,)),
        ],
        compiler_params=pltpu.CompilerParams(
            collective_id=0, has_side_effects=True, vmem_limit_bytes=VMEM_LIMIT
        ),
        name="main",
    )(owner, node, cell, weight, normal, source, diag, coupling, flux, density, momentum, adjoint, objective)


def update_kernel(
    back, owner_ref, rank_ref, cell_ref, plane_ref, middle, shell, out, shell_out, wide, acc_ref, result, passing, nodes, sems
):
    taken = [
        pltpu.make_async_copy(middle.at[0:4], passing, sems.at[0]),
        pltpu.make_async_copy(shell, nodes, sems.at[1]),
    ]
    given = [
        pltpu.make_async_copy(passing, out.at[0:4], sems.at[2]),
        pltpu.make_async_copy(nodes, shell_out, sems.at[3]),
        pltpu.make_async_copy(result, out.at[4], sems.at[4]),
    ]
    for copy in taken:
        copy.start()
    turned = back[...].reshape(128, 128).T
    high, low = split(jnp.concatenate([turned[0:64], turned[64:128]], 1))
    wide[0:64, :] = high.astype(bf16)
    wide[64:128, :] = low.astype(bf16)
    acc_ref[...] = jnp.zeros_like(acc_ref)

    def face_step(block, _):
        @pl.when(block == 1)
        def _():
            for k in range(2):
                taken[k].wait()
                given[k].start()

        at = pl.ds(pl.multiple_of(block * CHUNK, CHUNK), CHUNK)
        picked = dot(wide[...], as_bf16(one_hot(256, owner_column(owner_ref[:, at]))))
        within = one_hot(64, rank_ref[:, at])
        value = jnp.sum(jnp.where(within, picked[:64] + picked[64:], 0.0), 0, keepdims=True)
        first, second = split(value)
        cell = cell_ref[:, at]
        across = one_hot(SP, cell % SP)
        stacked = jnp.concatenate(
            [jnp.where(across, first, 0.0).astype(bf16), jnp.where(across, second, 0.0).astype(bf16)], 0
        )
        acc_ref[...] += dot_nt(as_bf16(one_hot(CX * CZ, cell // SP)), stacked)
        return 0

    lax.fori_loop(0, FACES // CHUNK, face_step, 0)
    result[...] = (plane_ref[...] + acc_ref[:, :128] + acc_ref[:, 128:]).reshape(CX, CZ, SP)
    given[2].start()
    for copy in given:
        copy.wait()


def update(back, owner, rank, cell, plane, middle, shell):
    hbm = pl.BlockSpec(memory_space=pl.ANY)
    return pl.pallas_call(
        update_kernel,
        out_shape=(
            jax.ShapeDtypeStruct((5, CX, CZ, SP), f32),
            jax.ShapeDtypeStruct((64, 3, 128), f32),
        ),
        in_specs=[vmem()] * 5 + [hbm] * 2,
        out_specs=(hbm, hbm),
        scratch_shapes=[
            pltpu.VMEM((128, 256), bf16),
            pltpu.VMEM((512, 256), f32),
            pltpu.VMEM((CX, CZ, SP), f32),
            pltpu.VMEM((4, CX, CZ, SP), f32),
            pltpu.VMEM((64, 3, 128), f32),
            pltpu.SemaphoreType.DMA((5,)),
        ],
        compiler_params=pltpu.CompilerParams(vmem_limit_bytes=VMEM_LIMIT),
        name="update",
    )(back, owner, rank, cell, plane, middle, shell)


def body(
    density, momentum, adjoint, objective, flux_jac, wall_owner, wall_node, wall_cell,
    wall_weight, wall_normal, shell_source, shell_diag, shell_coupling,
):
    owner = wall_owner.reshape(1, FACES)
    node = wall_node.reshape(1, FACES)
    cell = wall_cell.reshape(1, FACES)
    weight = wall_weight.reshape(1, FACES)
    source = shell_source.reshape(3, 64, 128).transpose(1, 0, 2)
    diag = shell_diag.reshape(3, 64, 128).transpose(1, 0, 2)
    coupling = shell_coupling.reshape(3, 3, 64, 128).transpose(0, 2, 1, 3)
    back, rank, plane, shell, middle = main_part(
        owner, node, cell, weight, wall_normal, source, diag, coupling,
        flux_jac.transpose(1, 0, 2), density, momentum, adjoint, objective,
    )
    fluid_out, shell = update(back, owner, rank, cell, plane, middle, shell)
    return fluid_out, shell.transpose(1, 0, 2).reshape(3, NODES)


def solution(mesh):
    wall = ("gx", "gz", "col")
    return jax.shard_map(
        body,
        mesh=mesh,
        in_specs=(
            P(*wall),
            P(None, *wall),
            P(None, *wall),
            P(None, *wall),
            P(),
            P(wall, None),
            P(wall),
            P(wall),
            P(wall),
            P(None, wall),
            P(None, wall),
            P(None, wall),
            P(None, None, wall),
        ),
        out_specs=(P(None, *wall), P(None, wall)),
        check_vma=False,
    )
```

```python
import functools

import jax
import jax.numpy as jnp
from jax import lax
from jax.experimental import pallas as pl
from jax.experimental.pallas import tpu as pltpu
from jax.sharding import PartitionSpec as P

tau = 0.25
f32, bf16, i32 = jnp.float32, jnp.bfloat16, jnp.int32
MESH = pl.DeviceIdType.MESH
GX, GZ, COL = 8, 16, 2
CX, CZ, SP = 32, 16, 128
FACES, NODES = 8192, 8192
ZB = 8
CHUNK = 2048
VMEM_LIMIT = 56 * 1024 * 1024


def vmem():
    return pl.BlockSpec(memory_space=pltpu.VMEM)


def part(block):
    return pl.ds(pl.multiple_of(block * CHUNK, CHUNK), CHUNK)


def split(x):
    high = x.astype(bf16).astype(f32)
    return high, x - high


def one_hot(rows, index):
    return lax.broadcasted_iota(i32, (rows, index.shape[1]), 0) == index


def as_bf16(mask):
    return jnp.where(mask, 1.0, 0.0).astype(bf16)


def dot(a, b):
    return jnp.dot(a, b, preferred_element_type=f32)


def dot_nt(a, b):
    return lax.dot_general(a, b, (((1,), (1,)), ((), ())), preferred_element_type=f32)


def owner_column(owner):
    return (owner % 2) * 128 + owner // 2


def slots_from(summed):
    return jnp.concatenate([summed[:, :128], summed[:, 128:]], 0).T


def place():
    return lax.axis_index("gx"), lax.axis_index("gz"), lax.axis_index("col")


def greet(gx, gz, col):
    barrier = pltpu.get_barrier_semaphore()
    for k in range(1, GX):
        pl.semaphore_signal(barrier, inc=1, device_id=((gx + k) % GX, gz, col), device_id_type=MESH)
    for k in range(1, GZ):
        pl.semaphore_signal(barrier, inc=1, device_id=(gx, (gz + k) % GZ, col), device_id_type=MESH)
    pl.semaphore_signal(barrier, inc=1, device_id=(gx, gz, 1 - col), device_id_type=MESH)


def greeted():
    pl.semaphore_wait(pltpu.get_barrier_semaphore(), GX + GZ - 1)


def remote(src, dst, sems, k, device):
    return pltpu.make_async_remote_copy(
        src_ref=src,
        dst_ref=dst,
        send_sem=sems.at[0, k],
        recv_sem=sems.at[1, k],
        device_id=device,
        device_id_type=MESH,
    )


class Stage:
    def __init__(self, copies, local=None):
        self.copies, self.local = copies, local

    def start(self):
        for copy in self.copies:
            copy.start()
        if self.local is not None:
            self.local.start()
        return self

    def arrive(self):
        for copy in self.copies:
            copy.wait_recv()
        if self.local is not None:
            self.local.wait()

    def sent(self):
        for copy in self.copies:
            copy.wait_send()


def along_gx(here, source, target, sems, local):
    gx, gz, col = here
    return Stage(
        [
            remote(source((gx + k) % GX), target(gx), sems, k - 1, ((gx + k) % GX, gz, col))
            for k in range(1, GX)
        ],
        pltpu.make_async_copy(source(gx), target(gx), local),
    )


def along_gz(here, source, target, sems, local):
    gx, gz, col = here
    return Stage(
        [
            remote(source((gz + k) % GZ), target(gz), sems, k - 1, (gx, (gz + k) % GZ, col))
            for k in range(1, GZ)
        ],
        pltpu.make_async_copy(source(gz), target(gz), local),
    )


def along_col(here, source, target, sems):
    gx, gz, col = here
    return Stage([remote(source, target, sems, 0, (gx, gz, 1 - col))])


def rank_faces(owner_ref, rank_ref, owners_ref, carry_ref):
    rows = lax.broadcasted_iota(i32, (256, 384), 0)
    cols = lax.broadcasted_iota(i32, (256, 384), 1)
    ahead = as_bf16((rows < cols) | (cols >= 256))
    carry_ref[...] = jnp.zeros_like(carry_ref)

    def step(block, _):
        at = part(block)
        mask = one_hot(256, owner_column(owner_ref[:, at]))
        chosen = as_bf16(mask)
        owners_ref[:, at] = chosen
        carry = carry_ref[...]
        ranks = []
        for k in range(CHUNK // 256):
            counts = dot(chosen[:, k * 256 : k * 256 + 256], ahead)
            before = counts[:, :256] + jnp.concatenate([carry, carry], 1)
            ranks.append(
                jnp.sum(jnp.where(mask[:, k * 256 : k * 256 + 256], before, 0.0), 0, keepdims=True)
            )
            carry = carry + counts[:, 256:]
        rank_ref[:, at] = jnp.concatenate(ranks, 1).astype(i32)
        carry_ref[...] = carry
        return 0

    lax.fori_loop(0, FACES // CHUNK, step, 0)


def place_fixed(first, last, node_ref, weight_ref, normal_ref, rank_ref, owners_ref, acc_ref):
    if first == 0:
        acc_ref[...] = jnp.zeros_like(acc_ref)

    def step(block, _):
        at = part(block)
        within = one_hot(64, rank_ref[:, at])
        weight = weight_ref[:, at]
        node = node_ref[:, at]
        pieces = []
        for k in range(3):
            pieces += split(weight * normal_ref[k : k + 1, at])
        pieces += [((node // 128) * 128).astype(f32), (node % 128).astype(f32)]
        stacked = jnp.concatenate(
            [jnp.where(within, piece, 0.0).astype(bf16) for piece in pieces], 0
        )
        acc_ref[...] += dot_nt(stacked, owners_ref[:, at])
        return 0

    lax.fori_loop(first, last, step, 0)


def fixed_payload(acc_ref, pay):
    for k in range(4):
        pay[k] = slots_from(
            acc_ref[k * 128 : k * 128 + 64, :] + acc_ref[k * 128 + 64 : k * 128 + 128, :]
        ).reshape(GX, GZ, 128)


def pack_side(col, ext, packed):
    lane = lax.broadcasted_iota(i32, (CZ, SP), 1)
    lane = (lane + 2 + 126 * col) % SP
    for j in range(5):
        kept = ext[j, 2, ZB : ZB + CZ]
        for x in range(1, CX):
            moved = pltpu.roll(ext[j, x + 2, ZB : ZB + CZ], 2 * x, 1)
            kept = jnp.where(lane // 2 == x, moved, kept)
        packed[j] = kept


def stencil(here, flux, density, momentum, objective, side, middle, plane_ref, ext):
    gx, gz, col = here
    lane = lax.broadcasted_iota(i32, (CZ, SP), 1)
    s_low = (col > 0).astype(f32)
    s_high = (col < COL - 1).astype(f32)
    inner = slice(ZB, ZB + CZ)
    nothing = functools.partial(jnp.zeros, dtype=f32)

    @pl.when(gx == 0)
    def _():
        ext[:, 0:2, inner] = nothing((5, 2, CZ, SP))

    @pl.when(gx == GX - 1)
    def _():
        ext[:, CX + 2 : CX + 4, inner] = nothing((5, 2, CZ, SP))

    @pl.when(gz == 0)
    def _():
        ext[:, 2 : CX + 2, ZB - 2 : ZB] = nothing((5, CX, 2, SP))

    @pl.when(gz == GZ - 1)
    def _():
        ext[:, 2 : CX + 2, ZB + CZ : ZB + CZ + 2] = nothing((5, CX, 2, SP))

    def one_plane(x, sides):
        inverse = 1.0 / density[x]
        velocity = [momentum[d, x] * inverse for d in range(3)]
        totals = [12.0 * objective[i, x] for i in range(5)]
        for j in range(5):
            now = ext[j, x + 2, inner]
            near = ext[j, x + 1, inner] - ext[j, x + 3, inner]
            far = ext[j, x, inner] - ext[j, x + 4, inner]
            spread(totals, velocity, j, 0, 8.0 * near - far)
            near = ext[j, x + 2, ZB - 1 : ZB - 1 + CZ] - ext[j, x + 2, ZB + 1 : ZB + 1 + CZ]
            far = ext[j, x + 2, ZB - 2 : ZB - 2 + CZ] - ext[j, x + 2, ZB + 2 : ZB + 2 + CZ]
            spread(totals, velocity, j, 1, 8.0 * near - far)
            low_side, high_side = sides[j] * s_low, sides[j] * s_high
            near = pltpu.roll(jnp.where(lane >= SP - 1, low_side, now), 1, 1) - pltpu.roll(
                jnp.where(lane < 1, high_side, now), SP - 1, 1
            )
            far = pltpu.roll(jnp.where(lane >= SP - 2, low_side, now), 2, 1) - pltpu.roll(
                jnp.where(lane < 2, high_side, now), SP - 2, 1
            )
            spread(totals, velocity, j, 2, 8.0 * near - far)
        for i in range(5):
            value = ext[i, x + 2, inner] - (tau / 12.0) * totals[i]
            middle[i, x] = value
            if i == 4:
                plane_ref[pl.ds(pl.multiple_of(x * CZ, CZ), CZ), :] = value

    def spread(totals, velocity, j, d, delta):
        totals[j] = totals[j] + velocity[d] * delta
        for i in range(5):
            totals[i] = totals[i] + flux[j, d, i] * delta

    def step(block, sides):
        for k in range(PLANES):
            one_plane(PLANES * block + k, sides)
            sides = tuple(pltpu.roll(value, SP - 2, 1) for value in sides)
        return sides

    lax.fori_loop(0, CX // PLANES, step, tuple(side[j] for j in range(5)))


def split_plane(plane_ref, wide, acc_ref):
    high, low = split(plane_ref[...].T)
    wide[0:128, :] = high.astype(bf16)
    wide[128:256, :] = low.astype(bf16)
    acc_ref[0:128, :] = jnp.zeros((128, 256), f32)


def gather_pressure(first, last, cell_ref, rank_ref, owners_ref, wide, acc_ref):
    def step(block, _):
        at = part(block)
        picked = dot(wide[...], as_bf16(one_hot(CX * CZ, cell_ref[:, at] // SP)))
        across = one_hot(SP, cell_ref[:, at] % SP)
        high = jnp.sum(jnp.where(across, picked[:128], 0.0), 0, keepdims=True)
        low = jnp.sum(jnp.where(across, picked[128:], 0.0), 0, keepdims=True)
        within = one_hot(64, rank_ref[:, at])
        stacked = jnp.concatenate(
            [jnp.where(within, high, 0.0).astype(bf16), jnp.where(within, low, 0.0).astype(bf16)], 0
        )
        acc_ref[0:128, :] += dot_nt(stacked, owners_ref[:, at])
        return 0

    lax.fori_loop(first, last, step, 0)


def pressure_payload(acc_ref, pay):
    pay[...] = slots_from(acc_ref[0:64, :] + acc_ref[64:128, :]).reshape(GX, GZ, 128)


WAYS = 2
PLANES = 2


def combine(col, own, other):
    half = lax.broadcasted_iota(i32, own.shape, own.ndim - 1) // 64
    return jnp.where(half == col, own, pltpu.roll(other, 64, own.ndim - 1))


def compact(col, rows, target, first):
    for h in range(GZ // 2):
        target[first + h] = combine(col, rows[2 * h + col], rows[2 * h + 1 - col])


def fixed_rows(first, last, fixed, rows_ref):
    def step(h, _):
        for k in range(WAYS):
            g = WAYS * h + k
            node = row(fixed, g, 3).astype(i32)
            line = node // 128
            rows_ref[g] = as_bf16(one_hot(256, (line // 32) * 128 + node % 128))
        return 0

    lax.fori_loop(first, last, step, 0)


def row(fixed, g, k):
    return jnp.concatenate([fixed[g, x, k : k + 1, :] for x in range(GX)], 1)


def node_columns(fixed, g):
    return one_hot(32, (row(fixed, g, 3).astype(i32) // 128) % 32)


def add_loads(first, last, press, fixed, rows_ref, acc_ref):
    if first == 0:
        acc_ref[0:192, :] = jnp.zeros((192, 256), f32)

    def step(h, _):
        total = acc_ref[0:192, :]
        for k in range(WAYS):
            g = WAYS * h + k
            columns = node_columns(fixed, g)
            pressure = jnp.concatenate([press[g, x : x + 1, :] for x in range(GX)], 1)
            pieces = []
            for c in range(3):
                pieces += split(pressure * row(fixed, g, c))
            stacked = jnp.concatenate([jnp.where(columns, piece, 0.0).astype(bf16) for piece in pieces], 0)
            total = total + dot_nt(stacked, rows_ref[g])
        acc_ref[0:192, :] = total
        return 0

    lax.fori_loop(first, last, step, 0)


def solve_shell(acc_ref, source, diag, coupling, shell_ref, table):
    loads = []
    for k in range(3):
        both = acc_ref[k * 64 : k * 64 + 32, :] + acc_ref[k * 64 + 32 : k * 64 + 64, :]
        loads.append(jnp.concatenate([both[:, :128], both[:, 128:]], 0) + source[:, k, :])
    for i in range(3):
        value = diag[:, i, :] * loads[i]
        for j in range(3):
            value = value + coupling[i, :, j, :] * loads[j]
        shell_ref[:, i, :] = value
        wide = jnp.concatenate([value[0:32], value[32:64]], 1)
        high, low = split(wide)
        table[i * 64 : i * 64 + 32, :] = high.astype(bf16)
        table[i * 64 + 32 : i * 64 + 64, :] = low.astype(bf16)


def pick_answers(first, last, table, fixed, rows_ref, answers):
    def step(h, _):
        for k in range(WAYS):
            g = WAYS * h + k
            picked = dot(table[...], rows_ref[g])
            columns = node_columns(fixed, g)
            answer = jnp.zeros((1, GX * 128), f32)
            for c in range(3):
                both = picked[c * 64 : c * 64 + 32] + picked[c * 64 + 32 : c * 64 + 64]
                answer = answer + row(fixed, g, c) * jnp.sum(jnp.where(columns, both, 0.0), 0, keepdims=True)
            for x in range(GX):
                answers[g, x : x + 1, :] = answer[:, x * 128 : x * 128 + 128]
        return 0

    lax.fori_loop(first, last, step, 0)


def mix_answers(col, answers, other, mixed):
    for h in range(GZ // 2):
        mixed[2 * h + col] = combine(col, answers[h], other[h])
        mixed[2 * h + 1 - col] = combine(1 - col, other[h], answers[h])


def main_kernel(
    owner, node_hbm, cell_hbm, weight_hbm, normal_hbm, source_hbm, diag_hbm, coupling_hbm,
    flux_hbm, density_hbm, momentum_hbm, adjoint_hbm, objective_hbm,
    back, rank_hbm, plane_hbm, shell_hbm, middle_hbm,
    node, cell, weight, normal, source, diag, coupling, rank, plane, shell,
    flux, density, momentum, objective, ext, middle, packed, side,
    owners, carry, acc, wide, rows_ref, table,
    pay0, hop0, own0, other0, fixed, pay1, hop1, own1, other1, press, answers, other2, mixed, hop2,
    sems_h, sems_z, sems_g, sems_c, local, loads, stores,
):
    here = gx, gz, col = place()
    greet(gx, gz, col)
    staged = [
        pltpu.make_async_copy(source_ref, target, loads.at[k])
        for k, (source_ref, target) in enumerate(
            [
                (adjoint_hbm, ext.at[:, 2 : CX + 2, ZB : ZB + CZ]),
                (node_hbm, node),
                (weight_hbm, weight),
                (normal_hbm, normal),
                (cell_hbm, cell),
                (flux_hbm, flux),
                (density_hbm, density),
                (momentum_hbm, momentum),
                (objective_hbm, objective),
                (source_hbm, source),
                (diag_hbm, diag),
                (coupling_hbm, coupling),
            ]
        )
    ]
    for copy in staged:
        copy.start()
    rank_faces(owner, rank, owners, carry)
    staged[0].wait()
    pack_side(col, ext, packed)
    greeted()
    up, down = ((gx + 1) % GX, gz, col), ((gx + GX - 1) % GX, gz, col)
    high, low = (gx, (gz + 1) % GZ, col), (gx, (gz + GZ - 1) % GZ, col)
    planes, inner = slice(2, CX + 2), slice(ZB, ZB + CZ)
    halos = Stage(
        [
            remote(ext.at[:, planes, ZB + CZ - 2 : ZB + CZ], ext.at[:, planes, ZB - 2 : ZB], sems_h, 2, high),
            remote(ext.at[:, planes, ZB : ZB + 2], ext.at[:, planes, ZB + CZ : ZB + CZ + 2], sems_h, 3, low),
            remote(ext.at[:, CX : CX + 2, inner], ext.at[:, 0:2, inner], sems_h, 0, up),
            remote(ext.at[:, 2:4, inner], ext.at[:, CX + 2 : CX + 4, inner], sems_h, 1, down),
            remote(packed, side, sems_h, 4, (gx, gz, 1 - col)),
        ]
    ).start()
    for copy in staged[1:]:
        copy.wait()
    place_fixed(0, 4, node, weight, normal, rank, owners, acc)
    fixed_payload(acc, pay0)
    fixed_z = along_gx(here, lambda x: pay0.at[:, x], lambda x: hop0.at[x], sems_z.at[0], local.at[0]).start()
    halos.arrive()
    stencil(here, flux, density, momentum, objective, side, middle, plane, ext)
    written = [
        pltpu.make_async_copy(middle, middle_hbm, stores.at[0]),
        pltpu.make_async_copy(plane, plane_hbm, stores.at[1]),
        pltpu.make_async_copy(rank, rank_hbm, stores.at[2]),
    ]
    for copy in written:
        copy.start()
    split_plane(plane, wide, acc)
    gather_pressure(0, 3, cell, rank, owners, wide, acc)
    fixed_z.arrive()
    fixed_g = along_gz(here, lambda z: hop0.at[:, :, z], lambda z: own0.at[z], sems_g.at[0], local.at[1]).start()
    gather_pressure(3, 4, cell, rank, owners, wide, acc)
    pressure_payload(acc, pay1)
    press_z = along_gx(here, lambda x: pay1.at[x], lambda x: hop1.at[x], sems_z.at[1], local.at[2]).start()
    press_z.arrive()
    press_g = along_gz(here, lambda z: hop1.at[:, z], lambda z: own1.at[z], sems_g.at[1], local.at[3]).start()
    half = GZ // WAYS // 2
    fixed_g.arrive()
    fixed_c = along_col(here, own0, other0, sems_c.at[0]).start()
    compact(col, own0, fixed, 0)
    fixed_rows(0, half, fixed, rows_ref)
    fixed_c.arrive()
    compact(col, other0, fixed, GZ // 2)
    fixed_rows(half, 2 * half, fixed, rows_ref)
    press_g.arrive()
    press_c = along_col(here, own1, other1, sems_c.at[1]).start()
    compact(col, own1, press, 0)
    add_loads(0, half, press, fixed, rows_ref, acc)
    press_c.arrive()
    compact(col, other1, press, GZ // 2)
    add_loads(half, 2 * half, press, fixed, rows_ref, acc)
    solve_shell(acc, source, diag, coupling, shell, table)
    written.append(pltpu.make_async_copy(shell, shell_hbm, stores.at[3]))
    written[3].start()
    pick_answers(half, 2 * half, table, fixed, rows_ref, answers)
    back_c = along_col(here, answers.at[GZ // 2 : GZ], other2, sems_c.at[2]).start()
    pick_answers(0, half, table, fixed, rows_ref, answers)
    back_c.arrive()
    mix_answers(col, answers, other2, mixed)
    back_g = along_gz(here, lambda z: mixed.at[z], lambda z: hop2.at[:, z], sems_g.at[2], local.at[4]).start()
    back_g.arrive()
    back_z = along_gx(here, lambda x: hop2.at[x], lambda x: back.at[x], sems_z.at[2], local.at[5]).start()
    back_z.arrive()
    for copy in written:
        copy.wait()
    for stage in (halos, fixed_z, fixed_g, fixed_c, press_z, press_g, press_c, back_c, back_g, back_z):
        stage.sent()


def main_part(owner, node, cell, weight, normal, source, diag, coupling, flux, density, momentum, adjoint, objective):
    hbm = pl.BlockSpec(memory_space=pl.ANY)
    dma = pltpu.SemaphoreType.DMA
    block = (5, CX, CZ, SP)
    return pl.pallas_call(
        main_kernel,
        out_shape=(
            jax.ShapeDtypeStruct((GX, GZ, 128), f32),
            jax.ShapeDtypeStruct((1, FACES), i32),
            jax.ShapeDtypeStruct((CX * CZ, SP), f32),
            jax.ShapeDtypeStruct((64, 3, 128), f32),
            jax.ShapeDtypeStruct(block, f32),
        ),
        in_specs=[vmem()] + [hbm] * 12,
        out_specs=(vmem(),) + (hbm,) * 4,
        scratch_shapes=[
            pltpu.VMEM((1, FACES), i32),
            pltpu.VMEM((1, FACES), i32),
            pltpu.VMEM((1, FACES), f32),
            pltpu.VMEM((3, FACES), f32),
            pltpu.VMEM((64, 3, 128), f32),
            pltpu.VMEM((64, 3, 128), f32),
            pltpu.VMEM((3, 64, 3, 128), f32),
            pltpu.VMEM((1, FACES), i32),
            pltpu.VMEM((CX * CZ, SP), f32),
            pltpu.VMEM((64, 3, 128), f32),
            pltpu.SMEM((5, 3, 5), f32),
            pltpu.VMEM((CX, CZ, SP), f32),
            pltpu.VMEM((3, CX, CZ, SP), f32),
            pltpu.VMEM(block, f32),
            pltpu.VMEM((5, CX + 4, 2 * ZB + CZ, SP), f32),
            pltpu.VMEM(block, f32),
            pltpu.VMEM((5, CZ, SP), f32),
            pltpu.VMEM((5, CZ, SP), f32),
            pltpu.VMEM((256, FACES), bf16),
            pltpu.VMEM((256, 128), f32),
            pltpu.VMEM((512, 256), f32),
            pltpu.VMEM((256, 512), bf16),
            pltpu.VMEM((GZ, 256, GX * 128), bf16),
            pltpu.VMEM((192, 256), bf16),
            pltpu.VMEM((4, GX, GZ, 128), f32),
            pltpu.VMEM((GX, 4, GZ, 128), f32),
            pltpu.VMEM((GZ, GX, 4, 128), f32),
            pltpu.VMEM((GZ, GX, 4, 128), f32),
            pltpu.VMEM((GZ, GX, 4, 128), f32),
            pltpu.VMEM((GX, GZ, 128), f32),
            pltpu.VMEM((GX, GZ, 128), f32),
            pltpu.VMEM((GZ, GX, 128), f32),
            pltpu.VMEM((GZ, GX, 128), f32),
            pltpu.VMEM((GZ, GX, 128), f32),
            pltpu.VMEM((GZ, GX, 128), f32),
            pltpu.VMEM((GZ // 2, GX, 128), f32),
            pltpu.VMEM((GZ, GX, 128), f32),
            pltpu.VMEM((GX, GZ, 128), f32),
            dma((2, 5)),
            dma((3, 2, GX - 1)),
            dma((3, 2, GZ - 1)),
            dma((3, 2, 1)),
            dma((6,)),
            dma((12,)),
            dma((4,)),
        ],
        compiler_params=pltpu.CompilerParams(
            collective_id=0, has_side_effects=True, vmem_limit_bytes=VMEM_LIMIT
        ),
        name="main",
    )(owner, node, cell, weight, normal, source, diag, coupling, flux, density, momentum, adjoint, objective)


def update_kernel(
    back, owner_ref, rank_ref, cell_ref, plane_ref, middle, shell, out, shell_out, wide, acc_ref, result, passing, nodes, sems
):
    taken = [
        pltpu.make_async_copy(middle.at[0:4], passing, sems.at[0]),
        pltpu.make_async_copy(shell, nodes, sems.at[1]),
    ]
    given = [
        pltpu.make_async_copy(passing, out.at[0:4], sems.at[2]),
        pltpu.make_async_copy(nodes, shell_out, sems.at[3]),
        pltpu.make_async_copy(result, out.at[4], sems.at[4]),
    ]
    for copy in taken:
        copy.start()
    turned = back[...].reshape(128, 128).T
    high, low = split(jnp.concatenate([turned[0:64], turned[64:128]], 1))
    wide[0:64, :] = high.astype(bf16)
    wide[64:128, :] = low.astype(bf16)
    acc_ref[...] = jnp.zeros_like(acc_ref)

    def face_step(block, _):
        @pl.when(block == 1)
        def _():
            for k in range(2):
                taken[k].wait()
                given[k].start()

        at = part(block)
        picked = dot(wide[...], as_bf16(one_hot(256, owner_column(owner_ref[:, at]))))
        within = one_hot(64, rank_ref[:, at])
        value = jnp.sum(jnp.where(within, picked[:64] + picked[64:], 0.0), 0, keepdims=True)
        first, second = split(value)
        cell = cell_ref[:, at]
        across = one_hot(SP, cell % SP)
        stacked = jnp.concatenate(
            [jnp.where(across, first, 0.0).astype(bf16), jnp.where(across, second, 0.0).astype(bf16)], 0
        )
        acc_ref[...] += dot_nt(as_bf16(one_hot(CX * CZ, cell // SP)), stacked)
        return 0

    lax.fori_loop(0, FACES // CHUNK, face_step, 0)
    result[...] = (plane_ref[...] + acc_ref[:, :128] + acc_ref[:, 128:]).reshape(CX, CZ, SP)
    given[2].start()
    for copy in given:
        copy.wait()


def update(back, owner, rank, cell, plane, middle, shell):
    hbm = pl.BlockSpec(memory_space=pl.ANY)
    return pl.pallas_call(
        update_kernel,
        out_shape=(
            jax.ShapeDtypeStruct((5, CX, CZ, SP), f32),
            jax.ShapeDtypeStruct((64, 3, 128), f32),
        ),
        in_specs=[vmem()] * 5 + [hbm] * 2,
        out_specs=(hbm, hbm),
        scratch_shapes=[
            pltpu.VMEM((128, 256), bf16),
            pltpu.VMEM((512, 256), f32),
            pltpu.VMEM((CX, CZ, SP), f32),
            pltpu.VMEM((4, CX, CZ, SP), f32),
            pltpu.VMEM((64, 3, 128), f32),
            pltpu.SemaphoreType.DMA((5,)),
        ],
        compiler_params=pltpu.CompilerParams(vmem_limit_bytes=VMEM_LIMIT),
        name="update",
    )(back, owner, rank, cell, plane, middle, shell)


def body(
    density, momentum, adjoint, objective, flux_jac, wall_owner, wall_node, wall_cell,
    wall_weight, wall_normal, shell_source, shell_diag, shell_coupling,
):
    owner = wall_owner.reshape(1, FACES)
    node = wall_node.reshape(1, FACES)
    cell = wall_cell.reshape(1, FACES)
    weight = wall_weight.reshape(1, FACES)
    source = shell_source.reshape(3, 64, 128).transpose(1, 0, 2)
    diag = shell_diag.reshape(3, 64, 128).transpose(1, 0, 2)
    coupling = shell_coupling.reshape(3, 3, 64, 128).transpose(0, 2, 1, 3)
    back, rank, plane, shell, middle = main_part(
        owner, node, cell, weight, wall_normal, source, diag, coupling,
        flux_jac.transpose(1, 0, 2), density, momentum, adjoint, objective,
    )
    fluid_out, shell = update(back, owner, rank, cell, plane, middle, shell)
    return fluid_out, shell.transpose(1, 0, 2).reshape(3, NODES)


def solution(mesh):
    wall = ("gx", "gz", "col")
    return jax.shard_map(
        body,
        mesh=mesh,
        in_specs=(
            P(*wall),
            P(None, *wall),
            P(None, *wall),
            P(None, *wall),
            P(),
            P(wall, None),
            P(wall),
            P(wall),
            P(wall),
            P(None, wall),
            P(None, wall),
            P(None, wall),
            P(None, None, wall),
        ),
        out_specs=(P(None, *wall), P(None, wall)),
        check_vma=False,
    )
```
